256 devices in a mesh: lat: 4 (over y_hi, core), lon: 32 (over x, z), lev: 2 (over y_lo).
Axes of the slice: x: 4, y: 4 (y_hi: 2, y_lo: 2; y = y_hi * 2 + y_lo), z: 8, core: 2. Of those that a mesh axis runs over, the one named last changes fastest.
Arguments:
- levels_in: bfloat16 [4, 24, 768, 512], P('lev', 'lat', 'lon'), may hold values from -150 to 150, as said below
- enc_gain: bfloat16 [512], replicated, may hold values from 0.099609375 to 1.8984375
- latent_query: bfloat16 [2, 512], replicated, may hold values from -6 to 6
- w_query: bfloat16 [512, 512], replicated, may hold values from -16 to 16
- w_kv: bfloat16 [512, 1024], replicated, may hold values from -0.25 to 0.25
- w_cross_out: bfloat16 [512, 512], replicated, may hold values from -0.25 to 0.25
- shift_lat: int32 [1], replicated, may hold values from 0 to 5
- shift_lon: int32 [1], replicated, may hold values from 0 to 11
- attn_gain: bfloat16 [512], replicated, may hold values from 0.099609375 to 1.8984375
- w_qkv: bfloat16 [512, 1536], replicated, may hold values from -16 to 16
- w_proj: bfloat16 [512, 512], replicated, may hold values from -0.25 to 0.25
- mlp_gain: bfloat16 [512], replicated, may hold values from 0.099609375 to 1.8984375
- w_up: bfloat16 [512, 2048], replicated, may hold values from -0.25 to 0.25
- w_down: bfloat16 [2048, 512], replicated, may hold values from -0.125 to 0.125
- merge_gain: bfloat16 [2048], replicated, may hold values from 0.099609375 to 1.8984375
- w_merge: bfloat16 [2048, 1024], replicated, may hold values from -0.125 to 0.125
Outputs:
- merged: bfloat16 [2, 12, 384, 1024], P(None, 'lat', ('lon', 'lev'))
The draws below stay inside these ranges and needn't reach their ends.
Inputs may be any that keep to these rules, and one draw needn't show every extreme that they name: `levels_in`: level tokens of varying magnitude from token to token and from feature to feature.
All inputs are finite; a program needn't handle non-finite values.
Results may differ from the reference program's by a relative error of at most 0.015.
The reference program's roundings to bfloat16 on the way count: a program that leaves them out, or rounds other values in their place, can miss the bound.
Values may be sent and summed in bfloat16 or wider, within the bound.
No kernel may reach another device: no remote copies, remote signals or barrier semaphores. Data moves between devices by JAX's collectives and lax.ppermute only.
A program may use at most 128 MiB of HBM per device.

```python
import math
import jax
import jax.numpy as jnp
from jax import lax

D = 512
FF = 2048
HEADS = 16
WH = 6
WW = 12
LATENT = 2
LEVELS = 4
NR = 24
NC = 768


def draw_levels_in(key, part):
    key = jax.random.fold_in(key, 5)
    key_noise, key_token, key_feature = jax.random.split(key, 3)
    full_shape = (LEVELS, NR, NC, D)
    noise_draw = jnp.clip(jax.random.normal(key_noise, full_shape, jnp.float32), -6.0, 6.0)
    token_scale = jnp.exp(jax.random.uniform(key_token, (LEVELS, NR, NC, 1), jnp.float32, 0.0, math.log(10.0)))
    feature_scale = jnp.exp(jax.random.uniform(key_feature, (D,), jnp.float32, math.log(0.3), math.log(3.0)))
    values = noise_draw * token_scale * feature_scale / 3.0
    return values.astype(jnp.bfloat16)


def draw_w_query(key, part):
    key = jax.random.fold_in(key, 11)
    matrix = jnp.clip(jax.random.normal(key, (D, D), jnp.float32), -6.0, 6.0) * D ** (-0.5)
    return matrix.astype(jnp.bfloat16)


def draw_w_qkv(key, part):
    key = jax.random.fold_in(key, 23)
    matrix = jnp.clip(jax.random.normal(key, (D, 3 * D), jnp.float32), -6.0, 6.0) * D ** (-0.5)
    return matrix.astype(jnp.bfloat16)


def normal_values(stream_key, shape, width, most, kind=jnp.bfloat16):
    return jnp.clip(width * jax.random.normal(stream_key, shape, jnp.float32), -most, most).astype(kind)


def setup_inputs(seed: int = 0) -> dict:
    key_of = jax.random.split(jax.random.key(seed), 17)
    return {
        "levels_in": draw_levels_in(jax.random.fold_in(key_of[16], 71), 0),
        "enc_gain": jnp.clip(1.0 + 0.18 * jax.random.normal(key_of[1], (D,), jnp.float32), 0.099609375, 1.8984375).astype(jnp.bfloat16),
        "latent_query": normal_values(key_of[2], (LATENT, D), 1.0, 6.0),
        "w_query": draw_w_query(jax.random.fold_in(key_of[16], 71), 0),
        "w_kv": normal_values(key_of[4], (D, 2 * D), D ** -0.5, 0.25),
        "w_cross_out": normal_values(key_of[5], (D, D), D ** -0.5, 0.25),
        "shift_lat": jax.random.randint(key_of[6], (1,), 0, WH).astype(jnp.int32),
        "shift_lon": jax.random.randint(key_of[7], (1,), 0, WW).astype(jnp.int32),
        "attn_gain": jnp.clip(1.0 + 0.18 * jax.random.normal(key_of[8], (D,), jnp.float32), 0.099609375, 1.8984375).astype(jnp.bfloat16),
        "w_qkv": draw_w_qkv(jax.random.fold_in(key_of[16], 71), 0),
        "w_proj": normal_values(key_of[10], (D, D), D ** -0.5, 0.25),
        "mlp_gain": jnp.clip(1.0 + 0.18 * jax.random.normal(key_of[11], (D,), jnp.float32), 0.099609375, 1.8984375).astype(jnp.bfloat16),
        "w_up": normal_values(key_of[12], (D, FF), D ** -0.5, 0.25),
        "w_down": normal_values(key_of[13], (FF, D), FF ** -0.5, 0.125),
        "merge_gain": jnp.clip(1.0 + 0.18 * jax.random.normal(key_of[14], (4 * D,), jnp.float32), 0.099609375, 1.8984375).astype(jnp.bfloat16),
        "w_merge": normal_values(key_of[15], (4 * D, 2 * D), (4 * D) ** -0.5, 0.125),
    }


EPSILON = 1e-05
NEG_LARGE = -1e+30

def layer_norm(values, gain_vec):
    values = values.astype(jnp.float32)
    centre = values - lax.optimization_barrier(jnp.mean(values, axis=-1, keepdims=True))
    spread = lax.optimization_barrier(jnp.mean(centre * centre, axis=-1, keepdims=True))
    return centre * lax.rsqrt(spread + EPSILON) * gain_vec.astype(jnp.float32)

def project(values, weight):
    lead_shape = values.shape[:-1]
    flat_rows = values.reshape(-1, values.shape[-1])
    product = jnp.dot(flat_rows, weight, preferred_element_type=jnp.float32)
    return product.reshape(lead_shape + (weight.shape[1],))

def widen(values):
    return lax.optimization_barrier(values.astype(jnp.bfloat16)).astype(jnp.float32)

def encode(tokens, enc_gain, queries, latent_query, w_kv, w_cross_out):
    level_count, row_total, col_total, feat_width = tokens.shape
    head_dim = feat_width // HEADS
    normed = layer_norm(tokens, enc_gain).astype(jnp.bfloat16)
    keyval = widen(project(normed, w_kv))
    key_part = keyval[..., :feat_width].reshape(level_count, row_total, col_total, HEADS, head_dim)
    value_part = keyval[..., feat_width:].reshape(level_count, row_total, col_total, HEADS, head_dim)
    query_heads = queries.astype(jnp.float32).reshape(-1, HEADS, head_dim)
    scores = jnp.einsum('khe,lrche->rchkl', query_heads, key_part) / math.sqrt(head_dim)
    weights = widen(jax.nn.softmax(scores, axis=-1))
    attended = jnp.einsum('rchkl,lrche->krche', weights, value_part)
    attended = attended.astype(jnp.bfloat16).reshape(-1, row_total, col_total, feat_width)
    latents = latent_query.astype(jnp.float32)[:, None, None, :] + project(attended, w_cross_out)
    return latents.astype(jnp.bfloat16)

def reference(levels_in, enc_gain, latent_query, w_query, w_kv, w_cross_out, shift_lat, shift_lon, attn_gain, w_qkv, w_proj, mlp_gain, w_up, w_down, merge_gain, w_merge):
    queries = jnp.dot(latent_query, w_query, preferred_element_type=jnp.float32).astype(jnp.bfloat16)
    latents = encode(levels_in, enc_gain, queries, latent_query, w_kv, w_cross_out)
    normed = layer_norm(latents, attn_gain).astype(jnp.bfloat16)
    qkv = project(normed, w_qkv).astype(jnp.bfloat16)
    shift_row = shift_lat[0].astype(jnp.int32)
    shift_col = shift_lon[0].astype(jnp.int32)
    rolled = jnp.roll(qkv, shift_col, axis=2)
    padded = jnp.pad(rolled, ((0, 0), (WH, WH), (0, 0), (0, 0)))
    spanned = lax.dynamic_slice_in_dim(padded, (WH - shift_row).astype(jnp.int32), NR + WH, 1)
    row_count = NR // WH + 1
    col_count = NC // WW
    head_dim = D // HEADS
    global_rows = jnp.arange(NR + WH, dtype=jnp.int32) - shift_row
    inside = (global_rows >= 0) & (global_rows < NR)
    row_labels = jnp.where(inside, 0, -1).astype(jnp.int32).reshape(row_count, WH)
    blocked = spanned.reshape(LATENT, row_count, WH, col_count, WW, 3 * D)
    blocked = blocked.transpose(1, 3, 0, 2, 4, 5).reshape(row_count, col_count, LATENT * WH * WW, 3 * D)

    def attend_row(inputs):
        window_block, label_row = inputs
        labels = jnp.broadcast_to(label_row[None, :, None], (LATENT, WH, WW)).reshape(-1)
        allowed = labels[:, None] == labels[None, :]
        window_block = window_block.astype(jnp.float32)
        token_count = window_block.shape[1]
        query_part = window_block[..., :D].reshape(col_count, token_count, HEADS, head_dim)
        key_part = window_block[..., D:2 * D].reshape(col_count, token_count, HEADS, head_dim)
        value_part = window_block[..., 2 * D:].reshape(col_count, token_count, HEADS, head_dim)
        scores = jnp.einsum('cqhe,ckhe->chqk', query_part, key_part) / math.sqrt(head_dim)
        scores = jnp.where(allowed[None, None], scores, NEG_LARGE)
        weights = widen(jax.nn.softmax(scores, axis=-1))
        output = jnp.einsum('chqk,ckhe->cqhe', weights, value_part)
        return output.astype(jnp.bfloat16).reshape(col_count, token_count, D)
    window_out = lax.map(attend_row, (blocked, row_labels))
    window_out = window_out.reshape(row_count, col_count, LATENT, WH, WW, D)
    window_out = window_out.transpose(2, 0, 3, 1, 4, 5).reshape(LATENT, NR + WH, NC, D)
    window_out = lax.dynamic_slice_in_dim(window_out, shift_row, NR, 1)
    window_out = jnp.roll(window_out, -shift_col, axis=2)
    middle = latents.astype(jnp.float32) + project(window_out, w_proj)
    mlp_in = layer_norm(middle, mlp_gain).astype(jnp.bfloat16)
    hidden = jax.nn.gelu(project(mlp_in, w_up)).astype(jnp.bfloat16)
    block_out = (middle + project(hidden, w_down)).astype(jnp.bfloat16)
    grouped = block_out.reshape(LATENT, NR // 2, 2, NC // 2, 2, D)
    grouped = grouped.transpose(0, 1, 3, 4, 2, 5).reshape(LATENT, NR // 2, NC // 2, 4 * D)
    merge_in = layer_norm(grouped, merge_gain).astype(jnp.bfloat16)
    return project(merge_in, w_merge).astype(jnp.bfloat16)
```

```python
import math

import jax
import jax.numpy as jnp
from jax import lax
from jax.experimental import pallas as pl
from jax.experimental.pallas import tpu as pltpu
from jax.sharding import PartitionSpec as P

HEADS = 16
WH = 6
WW = 12
LATENT = 2
D = 512
HD = D // HEADS
TOK = LATENT * WH * WW
EPSILON = 1e-05
NEG_LARGE = -1e30
F32 = jnp.float32
BF16 = jnp.bfloat16
SCALE = 1.0 / math.sqrt(HD)
AXES = ("lat", "lon", "lev")


def layer_norm(values, gain_row):
    centre = values - jnp.mean(values, axis=-1, keepdims=True)
    spread = jnp.mean(centre * centre, axis=-1, keepdims=True)
    return centre * lax.rsqrt(spread + EPSILON) * gain_row


def dot(a, b):
    return jnp.dot(a, b, preferred_element_type=F32)


def dot_t(a, b):
    return lax.dot_general(a, b, (((1,), (1,)), ((), ())), preferred_element_type=F32)


def iota(shape, dim):
    return lax.broadcasted_iota(jnp.int32, shape, dim)


def split(index, size):
    whole = jnp.floor((index.astype(F32) + 0.5) * (1.0 / size)).astype(jnp.int32)
    return whole, index - whole * size


def token_coords(index):
    level, rest = split(index, WH * WW)
    row, col = split(rest, WW)
    return level, row, col


def level_keyval(levels_ref, gain_row, w_kv):
    pieces = [
        levels_ref[l, r].astype(F32)
        for l in range(levels_ref.shape[0])
        for r in range(levels_ref.shape[1])
    ]
    normed = layer_norm(jnp.concatenate(pieces, axis=0), gain_row).astype(BF16)
    return dot(normed, w_kv).astype(BF16)


def local_kernel(levels_ref, gain_ref, lq_ref, wq_ref, wkv_ref, score_ref, value_ref, query_ref):
    queries = dot(lq_ref[...], wq_ref[...]).astype(BF16).astype(F32)
    rows = LATENT * HEADS
    spread = jnp.concatenate(
        [jnp.broadcast_to(queries[k : k + 1], (HEADS, D)) for k in range(LATENT)], axis=0
    )
    head_of_row = split(iota((rows, 1), 0), HEADS)[1]
    head_of_lane = split(iota((1, D), 1), HD)[0]
    query_rows = jnp.where(head_of_row == head_of_lane, spread, 0.0).astype(BF16)
    keyval = level_keyval(levels_ref, gain_ref[...].astype(F32), wkv_ref[...])
    score_ref[...] = dot_t(keyval[:, :D], query_rows)
    value_ref[...] = keyval[:, D:]
    query_ref[...] = query_rows


def encode_kernel(
    levels_ref, score_ref, value_ref, query_ref, gain_ref, lq_ref, wkv_ref, wcross_ref,
    both_ref, own_ref, other_ref,
):
    lev = lax.axis_index("lev")
    keyval = level_keyval(levels_ref, gain_ref[...].astype(F32), wkv_ref[...])
    far_scores = dot_t(keyval[:, :D], query_ref[...])
    near_scores = score_ref[...]
    count = near_scores.shape[0] // 2
    scores = [s[i * count : (i + 1) * count] * SCALE for s in (near_scores, far_scores) for i in (0, 1)]
    top = jnp.maximum(jnp.maximum(scores[0], scores[1]), jnp.maximum(scores[2], scores[3]))
    powers = [jnp.exp(s - top) for s in scores]
    norm = 1.0 / (powers[0] + powers[1] + powers[2] + powers[3])
    weights = jnp.concatenate([p * norm for p in powers], axis=0).astype(BF16)
    lane = iota((1, LATENT * D), 1)
    expand = (iota((LATENT * HEADS, 1), 0) == split(lane, HD)[0]).astype(F32).astype(BF16)
    wide = dot(weights, expand)
    near_values = value_ref[...].astype(F32)
    far_values = keyval[:, D:].astype(F32)
    values = [x[i * count : (i + 1) * count] for x in (near_values, far_values) for i in (0, 1)]
    attended = []
    for k in range(LATENT):
        total = 0.0
        for l in range(4):
            total = total + wide[l * count : (l + 1) * count, k * D : (k + 1) * D] * values[l]
        attended.append(total.astype(BF16))
    projected = dot(jnp.concatenate(attended, axis=0), wcross_ref[...])
    query = lq_ref[...].astype(F32)
    latents = jnp.concatenate(
        [projected[k * count : (k + 1) * count] + query[k : k + 1] for k in range(LATENT)], axis=0
    ).astype(BF16)
    half, rest = split(iota((2 * TOK, 1), 0), TOK)
    level, row, col = token_coords(rest)
    side = jnp.where(half == 0, lev, 1 - lev)
    source = level * count + row * (2 * WW) + col + side * WW
    order = (iota((1, 2 * TOK), 1) == source).astype(F32).astype(BF16)
    both = dot(order, latents).astype(BF16)
    both_ref[...] = both
    own_ref[...] = both[:TOK]
    other_ref[...] = both[TOK:]


def block_kernel(
    shift_lat_ref, shift_lon_ref, both_ref, far_ref, chip_ref, chip_far_ref, cross_ref,
    cross_far_ref, attn_gain_ref, wqkv_ref, wproj_ref, mlp_gain_ref, wup_ref, wdown_ref,
    merge_gain_ref, wmerge_ref, out_ref,
):
    lat = lax.axis_index("lat")
    lev = lax.axis_index("lev")
    last_lat = lax.axis_size("lat") - 1
    shift_row = shift_lat_ref[0]
    shift_col = shift_lon_ref[0]
    _, row, col = token_coords(iota((TOK, 1), 0))
    row_low = (row >= WH - shift_row).astype(jnp.int32)
    col_low = (col >= WW - shift_col).astype(jnp.int32)
    use_other = col_low == lev
    use_chip = row_low == lat % 2
    own = both_ref[:TOK].astype(F32)
    other = both_ref[TOK:].astype(F32)
    chip_own = chip_ref[:TOK].astype(F32)
    chip_other = chip_ref[TOK:].astype(F32)
    cross_other = cross_ref[:TOK].astype(F32)
    cross_own = cross_ref[TOK:].astype(F32)
    far = far_ref[...].astype(F32)
    chip_far = chip_far_ref[...].astype(F32)
    cross_far = cross_far_ref[...].astype(F32)
    beside = jnp.where(use_other, other, far)
    above = jnp.where(use_chip, chip_own, cross_own)
    corner = jnp.where(
        use_chip, jnp.where(use_other, chip_other, chip_far), jnp.where(use_other, cross_other, cross_far)
    )
    tokens = jnp.concatenate([own, beside, above, corner], axis=0)
    normed = layer_norm(tokens, attn_gain_ref[...].astype(F32)).astype(BF16)
    query = dot(normed[:TOK], wqkv_ref[:, :D]).astype(BF16)
    keyval = dot(normed, wqkv_ref[:, D:]).astype(BF16)

    group, rest = split(iota((1, 4 * TOK), 1), TOK)
    _, key_row, key_col = token_coords(rest)
    group_row, group_col = split(group, 2)
    key_row_low = (key_row >= WH - shift_row).astype(jnp.int32)
    key_col_low = (key_col >= WW - shift_col).astype(jnp.int32)
    key_label = (key_row_low ^ group_row) * 2 + (key_col_low ^ group_col)
    outside = (group_row == 1) & (
        ((lat == 0) & (key_row_low == 1)) | ((lat == last_lat) & (key_row_low == 0))
    )
    key_label = jnp.where(outside, -1, key_label)
    bias = jnp.where(row_low * 2 + col_low == key_label, 0.0, NEG_LARGE)

    lanes = 256
    per = lanes // HD
    head_of_lane = split(iota((1, lanes), 1), HD)[0]
    window_parts = []
    for g in range(D // lanes):
        query_g = query[:, g * lanes : (g + 1) * lanes]
        key_g = keyval[:, g * lanes : (g + 1) * lanes]
        value_g = keyval[:, D + g * lanes : D + (g + 1) * lanes]
        total = jnp.zeros((TOK, lanes), F32)
        for h in range(per):
            here = head_of_lane == h
            scores = dot_t(query_g * here.astype(F32).astype(BF16), key_g) * SCALE + bias
            powers = jnp.exp(scores - jnp.max(scores, axis=-1, keepdims=True))
            weights = (powers * (1.0 / jnp.sum(powers, axis=-1, keepdims=True))).astype(BF16)
            total = jnp.where(here, dot(weights, value_g), total)
        window_parts.append(total.astype(BF16))
    window_out = jnp.concatenate(window_parts, axis=1)

    middle = own + dot(window_out, wproj_ref[...])
    mlp_in = layer_norm(middle, mlp_gain_ref[...].astype(F32)).astype(BF16)
    up = dot(mlp_in, wup_ref[...])
    inner = math.sqrt(2.0 / math.pi) * (up + 0.044715 * (up * up * up))
    hidden = (0.5 * up * (1.0 + jnp.tanh(inner))).astype(BF16)
    block_out = (middle + dot(hidden, wdown_ref[...])).astype(BF16)

    groups = LATENT * WH // 2
    rows = 8 * groups
    corner_index, place = split(iota((4 * rows, 1), 0), rows)
    pair, col_pair = split(place, 8)
    level, row_pair = split(pair, WH // 2)
    corner_col, corner_row = split(corner_index, 2)
    source = level * (WH * WW) + (row_pair * 2 + corner_row) * WW + col_pair * 2 + corner_col
    source = jnp.where(col_pair < WW // 2, source, -1)
    order = (iota((1, TOK), 1) == source).astype(F32).astype(BF16)
    sorted_out = dot(order, block_out)
    grouped = jnp.concatenate([sorted_out[i * rows : (i + 1) * rows] for i in range(4)], axis=1)
    merge_in = layer_norm(grouped, merge_gain_ref[...].astype(F32)).astype(BF16)
    merged = dot(merge_in, wmerge_ref[...])
    for k in range(LATENT):
        for i in range(WH // 2):
            start = (k * (WH // 2) + i) * 8
            out_ref[k, i] = merged[start : start + WW // 2].astype(BF16)


VMEM_SPEC = pl.BlockSpec(memory_space=pltpu.VMEM)
SMEM_SPEC = pl.BlockSpec(memory_space=pltpu.SMEM)


def params(mib):
    return pltpu.CompilerParams(vmem_limit_bytes=mib * 2**20)


def pairs(lats, lons, target):
    chosen = []
    for lat in range(lats):
        for lon in range(lons):
            for lev in range(2):
                to_lat, to_lon, to_lev = target(lat, lon, lev)
                chosen.append(
                    ((lat * lons + lon) * 2 + lev, (to_lat * lons + to_lon % lons) * 2 + to_lev)
                )
    return chosen


def on_device(
    levels_in,
    enc_gain,
    latent_query,
    w_query,
    w_kv,
    w_cross_out,
    shift_lat,
    shift_lon,
    attn_gain,
    w_qkv,
    w_proj,
    mlp_gain,
    w_up,
    w_down,
    merge_gain,
    w_merge,
):
    lats = lax.axis_size("lat")
    lons = lax.axis_size("lon")

    def chip(lat):
        return lat ^ 1

    def cross(lat):
        return (lat + 1) % lats if lat % 2 else (lat - 1) % lats

    def aside(lon, lev):
        return (lon - 1, 1) if lev == 0 else (lon + 1, 0)

    level_pairs = pairs(lats, lons, lambda a, o, v: (a, o, 1 - v))
    far_pairs = pairs(lats, lons, lambda a, o, v: (a, o + 1 if v == 0 else o - 1, v))
    chip_pairs = pairs(lats, lons, lambda a, o, v: (chip(a), o, v))
    cross_pairs = pairs(lats, lons, lambda a, o, v: (cross(a), o, 1 - v))
    corner_pairs = pairs(lats, lons, lambda a, o, v: (cross(a),) + aside(o, v))

    enc_row = enc_gain.reshape(1, D)
    far_levels = lax.ppermute(levels_in, AXES, level_pairs)
    positions = levels_in.shape[0] * levels_in.shape[1] * levels_in.shape[2]
    scores, values, query_rows = pl.pallas_call(
        local_kernel,
        out_shape=(
            jax.ShapeDtypeStruct((positions, LATENT * HEADS), F32),
            jax.ShapeDtypeStruct((positions, D), BF16),
            jax.ShapeDtypeStruct((LATENT * HEADS, D), BF16),
        ),
        in_specs=[VMEM_SPEC] * 5,
        out_specs=(VMEM_SPEC,) * 3,
        compiler_params=params(24),
        name="local_levels",
    )(levels_in, enc_row, latent_query, w_query, w_kv)
    both, own, other = pl.pallas_call(
        encode_kernel,
        out_shape=(
            jax.ShapeDtypeStruct((2 * TOK, D), BF16),
            jax.ShapeDtypeStruct((TOK, D), BF16),
            jax.ShapeDtypeStruct((TOK, D), BF16),
        ),
        in_specs=[VMEM_SPEC] * 8,
        out_specs=(VMEM_SPEC,) * 3,
        compiler_params=params(24),
        name="encode",
    )(far_levels, scores, values, query_rows, enc_row, latent_query, w_kv, w_cross_out)
    far = lax.ppermute(other, AXES, far_pairs)
    cross_far = lax.ppermute(own, AXES, corner_pairs)
    cross_both = lax.ppermute(both, AXES, cross_pairs)
    chip_both = lax.ppermute(both, AXES, chip_pairs)
    chip_far = lax.ppermute(far, AXES, chip_pairs)
    return pl.pallas_call(
        block_kernel,
        out_shape=jax.ShapeDtypeStruct((LATENT, WH // 2, WW // 2, w_merge.shape[1]), BF16),
        in_specs=[SMEM_SPEC] * 2 + [VMEM_SPEC] * 14,
        out_specs=VMEM_SPEC,
        compiler_params=params(48),
        name="window_block",
    )(
        shift_lat, shift_lon, both, far, chip_both, chip_far, cross_both, cross_far,
        attn_gain.reshape(1, D), w_qkv, w_proj, mlp_gain.reshape(1, D), w_up, w_down,
        merge_gain.reshape(1, 4 * D), w_merge,
    )


def solution(mesh):
    in_specs = (P("lev", "lat", "lon", None),) + (P(),) * 15
    out_specs = P(None, "lat", ("lon", "lev"), None)
    return jax.shard_map(
        on_device, mesh=mesh, in_specs=in_specs, out_specs=out_specs, check_vma=False
    )
```

```python
import math

import jax
import jax.numpy as jnp
from jax import lax
from jax.experimental import pallas as pl
from jax.experimental.pallas import tpu as pltpu
from jax.sharding import PartitionSpec as P

HEADS = 16
WH = 6
WW = 12
LATENT = 2
D = 512
HD = D // HEADS
TOK = LATENT * WH * WW
EPSILON = 1e-05
NEG_LARGE = -1e30
F32 = jnp.float32
BF16 = jnp.bfloat16
SCALE = 1.0 / math.sqrt(HD)
LOG2E = math.log2(math.e)
AXES = ("lat", "lon", "lev")


def layer_norm(values, gain_row):
    centre = values - jnp.mean(values, axis=-1, keepdims=True)
    spread = jnp.mean(centre * centre, axis=-1, keepdims=True)
    return centre * lax.rsqrt(spread + EPSILON) * gain_row


def dot(a, b):
    return jnp.dot(a, b, preferred_element_type=F32)


def dot_t(a, b):
    return lax.dot_general(a, b, (((1,), (1,)), ((), ())), preferred_element_type=F32)


def iota(shape, dim):
    return lax.broadcasted_iota(jnp.int32, shape, dim)


def split(index, size):
    whole = jnp.floor((index.astype(F32) + 0.5) * (1.0 / size)).astype(jnp.int32)
    return whole, index - whole * size


def token_coords(index):
    level, rest = split(index, WH * WW)
    row, col = split(rest, WW)
    return level, row, col


def row_of(ref):
    return ref[...].astype(F32).reshape(1, ref.shape[0])


def level_keyval(levels_ref, gain_row, w_kv):
    pieces = [
        levels_ref[l, r].astype(F32)
        for l in range(levels_ref.shape[0])
        for r in range(levels_ref.shape[1])
    ]
    normed = layer_norm(jnp.concatenate(pieces, axis=0), gain_row).astype(BF16)
    return dot(normed, w_kv).astype(BF16)


def local_kernel(
    levels_hbm, gain_ref, lq_ref, wq_hbm, wkv_hbm, wqkv_hbm, wcross_hbm, wproj_hbm, wup_hbm,
    wdown_hbm, wmerge_hbm,
    score_ref, value_ref, query_ref, wq_t_ref, wv_t_ref, wk_ref, wkv_ref, wcross_ref, wproj_ref,
    wup_ref, wdown_ref, wmerge_ref,
    levels_ref, wq_ref, wqkv_ref, sems,
):
    moves = [
        (levels_hbm, levels_ref),
        (wkv_hbm, wkv_ref),
        (wq_hbm, wq_ref),
        (wqkv_hbm, wqkv_ref),
        (wcross_hbm, wcross_ref),
        (wproj_hbm, wproj_ref),
        (wup_hbm, wup_ref),
        (wdown_hbm, wdown_ref),
        (wmerge_hbm, wmerge_ref),
    ]
    copies = [
        pltpu.make_async_copy(source, target, sems.at[i])
        for i, (source, target) in enumerate(moves)
    ]
    for copy in copies:
        copy.start()
    copies[0].wait()
    copies[1].wait()
    keyval = level_keyval(levels_ref, row_of(gain_ref), wkv_ref[...])
    value_ref[...] = keyval[:, D:]
    copies[2].wait()
    queries = dot(lq_ref[...], wq_ref[...]).astype(BF16).astype(F32)
    rows = LATENT * HEADS
    spread = jnp.concatenate(
        [jnp.broadcast_to(queries[k : k + 1], (HEADS, D)) for k in range(LATENT)], axis=0
    )
    head_of_row = split(iota((rows, 1), 0), HEADS)[1]
    head_of_lane = split(iota((1, D), 1), HD)[0]
    query_rows = jnp.where(head_of_row == head_of_lane, spread, 0.0).astype(BF16)
    score_ref[...] = dot_t(keyval[:, :D], query_rows)
    query_ref[...] = query_rows
    copies[3].wait()
    wq_t_ref[...] = wqkv_ref[:, :D].astype(F32).T.astype(BF16)
    wk_ref[...] = wqkv_ref[:, D : 2 * D]
    wv_t_ref[...] = wqkv_ref[:, 2 * D :].astype(F32).T.astype(BF16)
    for copy in copies[4:]:
        copy.wait()


def encode_kernel(
    levels_ref, score_ref, value_ref, query_ref, gain_ref, lq_ref, wkv_ref, wcross_ref,
    both_ref, own_ref, other_ref,
):
    lev = lax.axis_index("lev")
    keyval = level_keyval(levels_ref, row_of(gain_ref), wkv_ref[...])
    far_scores = dot_t(keyval[:, :D], query_ref[...])
    near_scores = score_ref[...]
    count = near_scores.shape[0] // 2
    scores = [s[i * count : (i + 1) * count] * SCALE for s in (near_scores, far_scores) for i in (0, 1)]
    top = jnp.maximum(jnp.maximum(scores[0], scores[1]), jnp.maximum(scores[2], scores[3]))
    powers = [jnp.exp(s - top) for s in scores]
    norm = 1.0 / (powers[0] + powers[1] + powers[2] + powers[3])
    weights = jnp.concatenate([p * norm for p in powers], axis=0).astype(BF16)
    lane = iota((1, LATENT * D), 1)
    expand = (iota((LATENT * HEADS, 1), 0) == split(lane, HD)[0]).astype(F32).astype(BF16)
    wide = dot(weights, expand)
    near_values = value_ref[...].astype(F32)
    far_values = keyval[:, D:].astype(F32)
    values = [x[i * count : (i + 1) * count] for x in (near_values, far_values) for i in (0, 1)]
    attended = []
    for k in range(LATENT):
        total = 0.0
        for l in range(4):
            total = total + wide[l * count : (l + 1) * count, k * D : (k + 1) * D] * values[l]
        attended.append(total.astype(BF16))
    projected = dot(jnp.concatenate(attended, axis=0), wcross_ref[...])
    query = lq_ref[...].astype(F32)
    latents = jnp.concatenate(
        [projected[k * count : (k + 1) * count] + query[k : k + 1] for k in range(LATENT)], axis=0
    ).astype(BF16)
    half, rest = split(iota((2 * TOK, 1), 0), TOK)
    level, row, col = token_coords(rest)
    side = jnp.where(half == 0, lev, 1 - lev)
    source = level * count + row * (2 * WW) + col + side * WW
    order = (iota((1, 2 * TOK), 1) == source).astype(F32).astype(BF16)
    both = dot(order, latents).astype(BF16)
    both_ref[...] = both
    own_ref[...] = both[:TOK]
    other_ref[...] = both[TOK:]


def block_kernel(
    shift_lat_ref, shift_lon_ref, both_ref, far_ref, chip_ref, chip_far_ref, cross_ref,
    cross_far_ref, attn_gain_ref, wk_ref, wq_t_ref, wv_t_ref, wproj_ref, mlp_gain_ref, wup_ref,
    wdown_ref, merge_gain_ref, wmerge_ref, out_ref,
):
    lat = lax.axis_index("lat")
    lev = lax.axis_index("lev")
    last_lat = lax.axis_size("lat") - 1
    shift_row = shift_lat_ref[0]
    shift_col = shift_lon_ref[0]
    _, row, col = token_coords(iota((TOK, 1), 0))
    row_low = (row >= WH - shift_row).astype(jnp.int32)
    col_low = (col >= WW - shift_col).astype(jnp.int32)
    use_other = col_low == lev
    use_chip = row_low == lat % 2
    gain = row_of(attn_gain_ref)
    own = both_ref[:TOK].astype(F32)
    other = both_ref[TOK:].astype(F32)
    chip_own = chip_ref[:TOK].astype(F32)
    chip_other = chip_ref[TOK:].astype(F32)
    cross_other = cross_ref[:TOK].astype(F32)
    cross_own = cross_ref[TOK:].astype(F32)
    beside = jnp.where(use_other, other, far_ref[...].astype(F32))
    above = jnp.where(use_chip, chip_own, cross_own)
    corner = jnp.where(
        use_chip,
        jnp.where(use_other, chip_other, chip_far_ref[...].astype(F32)),
        jnp.where(use_other, cross_other, cross_far_ref[...].astype(F32)),
    )
    own_n, beside_n, above_n, corner_n = [
        layer_norm(x, gain) for x in (own, beside, above, corner)
    ]
    windows = []
    for a in range(2):
        for b in range(2):
            near = jnp.where(col_low == b, own_n, beside_n)
            away = jnp.where(col_low == b, above_n, corner_n)
            windows.append(jnp.where(row_low == a, near, away).astype(BF16))
    keys = dot(jnp.concatenate(windows, axis=0), wk_ref[...]).astype(BF16)
    values_t = [dot_t(wv_t_ref[...], x).astype(BF16) for x in windows]
    query_t = dot_t(wq_t_ref[...], own_n.astype(BF16)).astype(BF16)

    lanes = 256
    per = lanes // HD
    main = 128
    rest = TOK - main
    packed = per * TOK
    lane = iota((1, packed), 1)
    in_main = lane < per * main
    token = jnp.where(in_main, split(lane, main)[1], main + split(lane, rest)[1])
    _, token_row, token_col = token_coords(token)
    label_row = (token_row >= WH - shift_row).astype(jnp.int32)
    label = label_row * 2 + (token_col >= WW - shift_col).astype(jnp.int32)
    outside = ((lat == 0) & (label_row == 0) & (row_low == 1)) | (
        (lat == last_lat) & (label_row == 1) & (row_low == 0)
    )
    bias = jnp.where(outside, NEG_LARGE, 0.0)
    head_of_row = split(iota((lanes, 1), 0), HD)[0]
    rest_lane = iota((1, main), 1)
    rest_head, rest_token = split(rest_lane, rest)
    repeat = (iota((TOK, 1), 0) == main + rest_token).astype(F32).astype(BF16)
    fold = (split(iota((main, 1), 0), rest)[1] == rest_lane).astype(F32).astype(BF16)
    rest_mask = head_of_row == rest_head

    def pick(parts, which):
        return jnp.where(
            which < 2,
            jnp.where(which == 0, parts[0], parts[1]),
            jnp.where(which == 2, parts[2], parts[3]),
        )

    main_parts = []
    rest_parts = []
    for g in range(D // lanes):
        lo = g * lanes
        query_g = query_t[lo : lo + lanes]
        query_main = query_g[:, :main].astype(F32)
        blocks = [jnp.where(head_of_row == h, query_main, 0.0).astype(BF16) for h in range(per)]
        blocks.append(jnp.where(rest_mask, dot(query_g, repeat), 0.0).astype(BF16))
        scores_all = dot(keys[:, lo : lo + lanes], jnp.concatenate(blocks, axis=1))
        scores = pick([scores_all[w * TOK : (w + 1) * TOK] for w in range(4)], label) + bias
        powers = jnp.exp2((scores - jnp.max(scores, axis=0, keepdims=True)) * (SCALE * LOG2E))
        weights = (powers * (1.0 / jnp.sum(powers, axis=0, keepdims=True))).astype(BF16)
        for h in range(per):
            at = lo + h * HD
            stacked = jnp.concatenate([v[at : at + HD] for v in values_t], axis=0)
            result = dot(stacked, weights[:, h * main : (h + 1) * main])
            main_parts.append(
                pick([result[w * HD : (w + 1) * HD] for w in range(4)], label[:, :main])
            )
        stacked = jnp.concatenate([v[lo : lo + lanes] for v in values_t], axis=0)
        result = dot(stacked, weights[:, per * main :])
        picked = pick([result[w * lanes : (w + 1) * lanes] for w in range(4)], label[:, per * main :])
        rest_parts.append(dot(jnp.where(rest_mask, picked, 0.0).astype(BF16), fold))
    window_out = jnp.concatenate(
        [
            jnp.concatenate(main_parts, axis=0).T,
            jnp.concatenate(rest_parts, axis=0).T[:rest],
        ],
        axis=0,
    ).astype(BF16)

    middle = own + dot(window_out, wproj_ref[...])
    mlp_in = layer_norm(middle, row_of(mlp_gain_ref)).astype(BF16)
    up = dot(mlp_in, wup_ref[...])
    inner = math.sqrt(2.0 / math.pi) * (up + 0.044715 * (up * up * up))
    hidden = (0.5 * up * (1.0 + jnp.tanh(inner))).astype(BF16)
    block_out = (middle + dot(hidden, wdown_ref[...])).astype(BF16)

    count = (WH // 2) * (WW // 2) * LATENT
    rows = (count + 7) // 8 * 8
    corner_index, place = split(iota((4 * rows, 1), 0), rows)
    pair, level = split(place, LATENT)
    row_pair, col_pair = split(pair, WW // 2)
    corner_col, corner_row = split(corner_index, 2)
    source = level * (WH * WW) + (row_pair * 2 + corner_row) * WW + col_pair * 2 + corner_col
    source = jnp.where(place < count, source, -1)
    order = (iota((1, TOK), 1) == source).astype(F32).astype(BF16)
    sorted_out = dot(order, block_out)
    grouped = jnp.concatenate([sorted_out[i * rows : (i + 1) * rows] for i in range(4)], axis=1)
    merge_in = layer_norm(grouped, row_of(merge_gain_ref)).astype(BF16)
    merged = dot(merge_in, wmerge_ref[...])
    for i in range(WH // 2):
        for j in range(WW // 2):
            start = (i * (WW // 2) + j) * LATENT
            out_ref[i, j] = merged[start : start + LATENT].astype(BF16)


VMEM_SPEC = pl.BlockSpec(memory_space=pltpu.VMEM)
HBM_SPEC = pl.BlockSpec(memory_space=pltpu.HBM)
SMEM_SPEC = pl.BlockSpec(memory_space=pltpu.SMEM)


def in_hbm(x):
    return pltpu.with_memory_space_constraint(x, pltpu.HBM)


def params(mib):
    return pltpu.CompilerParams(vmem_limit_bytes=mib * 2**20)


def pairs(lats, lons, target):
    chosen = []
    for lat in range(lats):
        for lon in range(lons):
            for lev in range(2):
                to_lat, to_lon, to_lev = target(lat, lon, lev)
                chosen.append(
                    ((lat * lons + lon) * 2 + lev, (to_lat * lons + to_lon % lons) * 2 + to_lev)
                )
    return chosen


def on_device(
    levels_in,
    enc_gain,
    latent_query,
    w_query,
    w_kv,
    w_cross_out,
    shift_lat,
    shift_lon,
    attn_gain,
    w_qkv,
    w_proj,
    mlp_gain,
    w_up,
    w_down,
    merge_gain,
    w_merge,
):
    lats = lax.axis_size("lat")
    lons = lax.axis_size("lon")

    def chip(lat):
        return lat ^ 1

    def cross(lat):
        return (lat + 1) % lats if lat % 2 else (lat - 1) % lats

    def aside(lon, lev):
        return (lon - 1, 1) if lev == 0 else (lon + 1, 0)

    level_pairs = pairs(lats, lons, lambda a, o, v: (a, o, 1 - v))
    far_pairs = pairs(lats, lons, lambda a, o, v: (a, o + 1 if v == 0 else o - 1, v))
    chip_pairs = pairs(lats, lons, lambda a, o, v: (chip(a), o, v))
    cross_pairs = pairs(lats, lons, lambda a, o, v: (cross(a), o, 1 - v))
    corner_pairs = pairs(lats, lons, lambda a, o, v: (cross(a),) + aside(o, v))

    far_levels = lax.ppermute(levels_in, AXES, level_pairs)
    positions = levels_in.shape[0] * levels_in.shape[1] * levels_in.shape[2]
    kept = (w_kv, w_cross_out, w_proj, w_up, w_down, w_merge)
    scores, values, query_rows, wq_t, wv_t, wk, wkv, wcross, wproj, wup, wdown, wmerge = pl.pallas_call(
        local_kernel,
        out_shape=(
            pltpu.VMEM((positions, LATENT * HEADS), F32),
            pltpu.VMEM((positions, D), BF16),
            pltpu.VMEM((LATENT * HEADS, D), BF16),
        )
        + (pltpu.VMEM((D, D), BF16),) * 3
        + tuple(pltpu.VMEM(w.shape, BF16) for w in kept),
        in_specs=[HBM_SPEC] + [VMEM_SPEC] * 2 + [HBM_SPEC] * 8,
        out_specs=(VMEM_SPEC,) * 12,
        scratch_shapes=[
            pltpu.VMEM(levels_in.shape, BF16),
            pltpu.VMEM(w_query.shape, BF16),
            pltpu.VMEM(w_qkv.shape, BF16),
            pltpu.SemaphoreType.DMA((9,)),
        ],
        compiler_params=params(14),
        name="local_levels",
    )(
        in_hbm(levels_in), enc_gain, latent_query,
        *[in_hbm(w) for w in (w_query, w_kv, w_qkv, w_cross_out, w_proj, w_up, w_down, w_merge)],
    )
    both, own, other = pl.pallas_call(
        encode_kernel,
        out_shape=(
            jax.ShapeDtypeStruct((2 * TOK, D), BF16),
            jax.ShapeDtypeStruct((TOK, D), BF16),
            jax.ShapeDtypeStruct((TOK, D), BF16),
        ),
        in_specs=[VMEM_SPEC] * 8,
        out_specs=(VMEM_SPEC,) * 3,
        compiler_params=params(14),
        name="encode",
    )(far_levels, scores, values, query_rows, enc_gain, latent_query, wkv, wcross)
    far = lax.ppermute(other, AXES, far_pairs)
    cross_far = lax.ppermute(own, AXES, corner_pairs)
    cross_both = lax.ppermute(both, AXES, cross_pairs)
    chip_both = lax.ppermute(both, AXES, chip_pairs)
    chip_far = lax.ppermute(far, AXES, chip_pairs)
    merged = pl.pallas_call(
        block_kernel,
        out_shape=jax.ShapeDtypeStruct((WH // 2, WW // 2, LATENT, w_merge.shape[1]), BF16),
        in_specs=[SMEM_SPEC] * 2 + [VMEM_SPEC] * 16,
        out_specs=VMEM_SPEC,
        compiler_params=params(24),
        name="window_block",
    )(
        shift_lat, shift_lon, both, far, chip_both, chip_far, cross_both, cross_far,
        attn_gain, wk, wq_t, wv_t, wproj, mlp_gain, wup, wdown, merge_gain, wmerge,
    )
    return merged.transpose(2, 0, 1, 3)


def solution(mesh):
    in_specs = (P("lev", "lat", "lon", None),) + (P(),) * 15
    out_specs = P(None, "lat", ("lon", "lev"), None)
    return jax.shard_map(
        on_device, mesh=mesh, in_specs=in_specs, out_specs=out_specs, check_vma=False
    )
```

```python
import math

import jax
import jax.numpy as jnp
from jax import lax
from jax.experimental import pallas as pl
from jax.experimental.pallas import tpu as pltpu
from jax.sharding import PartitionSpec as P

HEADS = 16
WH = 6
WW = 12
LATENT = 2
D = 512
HD = D // HEADS
TOK = LATENT * WH * WW
EPSILON = 1e-05
NEG_LARGE = -1e30
F32 = jnp.float32
BF16 = jnp.bfloat16
SCALE = 1.0 / math.sqrt(HD)
LOG2E = math.log2(math.e)
AXES = ("lat", "lon", "lev")


def layer_norm(values, gain_row):
    centre = values - jnp.mean(values, axis=-1, keepdims=True)
    spread = jnp.mean(centre * centre, axis=-1, keepdims=True)
    return centre * lax.rsqrt(spread + EPSILON) * gain_row


def dot(a, b):
    return jnp.dot(a, b, preferred_element_type=F32)


def dot_t(a, b):
    return lax.dot_general(a, b, (((1,), (1,)), ((), ())), preferred_element_type=F32)


def iota(shape, dim):
    return lax.broadcasted_iota(jnp.int32, shape, dim)


def split(index, size):
    whole = jnp.floor((index.astype(F32) + 0.5) * (1.0 / size)).astype(jnp.int32)
    return whole, index - whole * size


def token_coords(index):
    level, rest = split(index, WH * WW)
    row, col = split(rest, WW)
    return level, row, col


def row_of(ref):
    return ref[...].astype(F32).reshape(1, ref.shape[0])


def level_keyval(levels_ref, gain_row, w_kv):
    pieces = [
        levels_ref[l, r].astype(F32)
        for l in range(levels_ref.shape[0])
        for r in range(levels_ref.shape[1])
    ]
    normed = layer_norm(jnp.concatenate(pieces, axis=0), gain_row).astype(BF16)
    return dot(normed, w_kv).astype(BF16)


def local_kernel(
    levels_hbm, gain_ref, lq_ref, wq_hbm, wkv_hbm, wqkv_hbm, wcross_hbm, wproj_hbm, wup_hbm,
    wdown_hbm, wmerge_hbm,
    score_ref, value_ref, query_ref, wq_t_ref, wv_t_ref, wk_ref, wkv_ref, wcross_ref, wproj_ref,
    wup_ref, wdown_ref, wmerge_ref,
    levels_ref, wq_ref, wqkv_ref, sems,
):
    moves = [
        (levels_hbm, levels_ref),
        (wkv_hbm, wkv_ref),
        (wq_hbm, wq_ref),
        (wqkv_hbm, wqkv_ref),
        (wcross_hbm, wcross_ref),
        (wproj_hbm, wproj_ref),
        (wup_hbm, wup_ref),
        (wdown_hbm, wdown_ref),
        (wmerge_hbm, wmerge_ref),
    ]
    copies = [
        pltpu.make_async_copy(source, target, sems.at[i])
        for i, (source, target) in enumerate(moves)
    ]
    for copy in copies:
        copy.start()
    copies[0].wait()
    copies[1].wait()
    keyval = level_keyval(levels_ref, row_of(gain_ref), wkv_ref[...])
    value_ref[...] = keyval[:, D:]
    copies[2].wait()
    queries = dot(lq_ref[...], wq_ref[...]).astype(BF16).astype(F32)
    rows = LATENT * HEADS
    spread = jnp.concatenate(
        [jnp.broadcast_to(queries[k : k + 1], (HEADS, D)) for k in range(LATENT)], axis=0
    )
    head_of_row = split(iota((rows, 1), 0), HEADS)[1]
    head_of_lane = split(iota((1, D), 1), HD)[0]
    query_rows = jnp.where(head_of_row == head_of_lane, spread, 0.0).astype(BF16)
    score_ref[...] = dot_t(keyval[:, :D], query_rows)
    query_ref[...] = query_rows
    copies[3].wait()
    wq_t_ref[...] = wqkv_ref[:, :D].astype(F32).T.astype(BF16)
    wk_ref[...] = wqkv_ref[:, D : 2 * D]
    wv_t_ref[...] = wqkv_ref[:, 2 * D :].astype(F32).T.astype(BF16)
    for copy in copies[4:]:
        copy.wait()


def encode_kernel(
    levels_ref, score_ref, value_ref, query_ref, gain_ref, lq_ref, wkv_ref, wcross_ref,
    both_ref,
):
    lev = lax.axis_index("lev")
    keyval = level_keyval(levels_ref, row_of(gain_ref), wkv_ref[...])
    far_scores = dot_t(keyval[:, :D], query_ref[...])
    near_scores = score_ref[...]
    count = near_scores.shape[0] // 2
    scores = [s[i * count : (i + 1) * count] * SCALE for s in (near_scores, far_scores) for i in (0, 1)]
    top = jnp.maximum(jnp.maximum(scores[0], scores[1]), jnp.maximum(scores[2], scores[3]))
    powers = [jnp.exp(s - top) for s in scores]
    norm = 1.0 / (powers[0] + powers[1] + powers[2] + powers[3])
    weights = jnp.concatenate([p * norm for p in powers], axis=0).astype(BF16)
    lane = iota((1, LATENT * D), 1)
    expand = (iota((LATENT * HEADS, 1), 0) == split(lane, HD)[0]).astype(F32).astype(BF16)
    wide = dot(weights, expand)
    near_values = value_ref[...].astype(F32)
    far_values = keyval[:, D:].astype(F32)
    values = [x[i * count : (i + 1) * count] for x in (near_values, far_values) for i in (0, 1)]
    attended = []
    for k in range(LATENT):
        total = 0.0
        for l in range(4):
            total = total + wide[l * count : (l + 1) * count, k * D : (k + 1) * D] * values[l]
        attended.append(total.astype(BF16))
    projected = dot(jnp.concatenate(attended, axis=0), wcross_ref[...])
    query = lq_ref[...].astype(F32)
    latents = jnp.concatenate(
        [projected[k * count : (k + 1) * count] + query[k : k + 1] for k in range(LATENT)], axis=0
    ).astype(BF16)
    half, rest = split(iota((2 * TOK, 1), 0), TOK)
    level, row, col = token_coords(rest)
    side = jnp.where(half == 0, lev, 1 - lev)
    source = level * count + row * (2 * WW) + col + side * WW
    order = (iota((1, 2 * TOK), 1) == source).astype(F32).astype(BF16)
    both = dot(order, latents).astype(BF16)
    both_ref[...] = both


def halves_kernel(both_ref, chip_ref, own_ref, other_ref):
    own_ref[...] = both_ref[:TOK]
    other_ref[...] = both_ref[TOK:]


def block_kernel(
    shift_lat_ref, shift_lon_ref, both_ref, far_ref, chip_ref, chip_far_ref, cross_ref,
    cross_far_ref, attn_gain_ref, wk_ref, wq_t_ref, wv_t_ref, wproj_ref, mlp_gain_ref, wup_ref,
    wdown_ref, merge_gain_ref, wmerge_ref, out_ref,
):
    lat = lax.axis_index("lat")
    lev = lax.axis_index("lev")
    last_lat = lax.axis_size("lat") - 1
    shift_row = shift_lat_ref[0]
    shift_col = shift_lon_ref[0]
    _, row, col = token_coords(iota((TOK, 1), 0))
    row_low = (row >= WH - shift_row).astype(jnp.int32)
    col_low = (col >= WW - shift_col).astype(jnp.int32)
    use_other = col_low == lev
    use_chip = row_low == lat % 2
    gain = row_of(attn_gain_ref)
    own = both_ref[:TOK].astype(F32)
    other = both_ref[TOK:].astype(F32)
    chip_own = chip_ref[:TOK].astype(F32)
    chip_other = chip_ref[TOK:].astype(F32)
    cross_other = cross_ref[:TOK].astype(F32)
    cross_own = cross_ref[TOK:].astype(F32)
    beside = jnp.where(use_other, other, far_ref[...].astype(F32))
    above = jnp.where(use_chip, chip_own, cross_own)
    corner = jnp.where(
        use_chip,
        jnp.where(use_other, chip_other, chip_far_ref[...].astype(F32)),
        jnp.where(use_other, cross_other, cross_far_ref[...].astype(F32)),
    )
    own_n, beside_n, above_n, corner_n = [
        layer_norm(x, gain) for x in (own, beside, above, corner)
    ]
    windows = []
    for a in range(2):
        for b in range(2):
            near = jnp.where(col_low == b, own_n, beside_n)
            away = jnp.where(col_low == b, above_n, corner_n)
            windows.append(jnp.where(row_low == a, near, away).astype(BF16))
    keys = dot(jnp.concatenate(windows, axis=0), wk_ref[...]).astype(BF16)
    values_t = [dot_t(wv_t_ref[...], x).astype(BF16) for x in windows]
    query_t = dot_t(wq_t_ref[...], own_n.astype(BF16)).astype(BF16)

    lanes = 256
    per = lanes // HD
    main = 128
    rest = TOK - main
    packed = per * TOK
    lane = iota((1, packed), 1)
    in_main = lane < per * main
    token = jnp.where(in_main, split(lane, main)[1], main + split(lane, rest)[1])
    _, token_row, token_col = token_coords(token)
    label_row = (token_row >= WH - shift_row).astype(jnp.int32)
    label = label_row * 2 + (token_col >= WW - shift_col).astype(jnp.int32)
    outside = ((lat == 0) & (label_row == 0) & (row_low == 1)) | (
        (lat == last_lat) & (label_row == 1) & (row_low == 0)
    )
    bias = jnp.where(outside, NEG_LARGE, 0.0)
    head_of_row = split(iota((lanes, 1), 0), HD)[0]
    rest_lane = iota((1, main), 1)
    rest_head, rest_token = split(rest_lane, rest)
    repeat = (iota((TOK, 1), 0) == main + rest_token).astype(F32).astype(BF16)
    fold = (split(iota((main, 1), 0), rest)[1] == rest_lane).astype(F32).astype(BF16)
    rest_mask = head_of_row == rest_head

    def pick(parts, which):
        return jnp.where(
            which < 2,
            jnp.where(which == 0, parts[0], parts[1]),
            jnp.where(which == 2, parts[2], parts[3]),
        )

    main_parts = []
    rest_parts = []
    for g in range(D // lanes):
        lo = g * lanes
        query_g = query_t[lo : lo + lanes]
        query_main = query_g[:, :main].astype(F32)
        blocks = [jnp.where(head_of_row == h, query_main, 0.0).astype(BF16) for h in range(per)]
        blocks.append(jnp.where(rest_mask, dot(query_g, repeat), 0.0).astype(BF16))
        scores_all = dot(keys[:, lo : lo + lanes], jnp.concatenate(blocks, axis=1))
        scores = pick([scores_all[w * TOK : (w + 1) * TOK] for w in range(4)], label) + bias
        powers = jnp.exp2((scores - jnp.max(scores, axis=0, keepdims=True)) * (SCALE * LOG2E))
        weights = (powers * (1.0 / jnp.sum(powers, axis=0, keepdims=True))).astype(BF16)
        for h in range(per):
            at = lo + h * HD
            stacked = jnp.concatenate([v[at : at + HD] for v in values_t], axis=0)
            result = dot(stacked, weights[:, h * main : (h + 1) * main])
            main_parts.append(
                pick([result[w * HD : (w + 1) * HD] for w in range(4)], label[:, :main])
            )
        stacked = jnp.concatenate([v[lo : lo + lanes] for v in values_t], axis=0)
        result = dot(stacked, weights[:, per * main :])
        picked = pick([result[w * lanes : (w + 1) * lanes] for w in range(4)], label[:, per * main :])
        rest_parts.append(dot(jnp.where(rest_mask, picked, 0.0).astype(BF16), fold))
    window_out = jnp.concatenate(
        [
            jnp.concatenate(main_parts, axis=0).T,
            jnp.concatenate(rest_parts, axis=0).T[:rest],
        ],
        axis=0,
    ).astype(BF16)

    middle = own + dot(window_out, wproj_ref[...])
    mlp_in = layer_norm(middle, row_of(mlp_gain_ref)).astype(BF16)
    up = dot(mlp_in, wup_ref[...])
    inner = math.sqrt(2.0 / math.pi) * (up + 0.044715 * (up * up * up))
    hidden = (0.5 * up * (1.0 + jnp.tanh(inner))).astype(BF16)
    block_out = (middle + dot(hidden, wdown_ref[...])).astype(BF16)

    count = (WH // 2) * (WW // 2) * LATENT
    rows = (count + 7) // 8 * 8
    corner_index, place = split(iota((4 * rows, 1), 0), rows)
    pair, level = split(place, LATENT)
    row_pair, col_pair = split(pair, WW // 2)
    corner_col, corner_row = split(corner_index, 2)
    source = level * (WH * WW) + (row_pair * 2 + corner_row) * WW + col_pair * 2 + corner_col
    source = jnp.where(place < count, source, -1)
    order = (iota((1, TOK), 1) == source).astype(F32).astype(BF16)
    sorted_out = dot(order, block_out)
    grouped = jnp.concatenate([sorted_out[i * rows : (i + 1) * rows] for i in range(4)], axis=1)
    merge_in = layer_norm(grouped, row_of(merge_gain_ref)).astype(BF16)
    merged = dot(merge_in, wmerge_ref[...])
    for i in range(WH // 2):
        for j in range(WW // 2):
            start = (i * (WW // 2) + j) * LATENT
            out_ref[i, j] = merged[start : start + LATENT].astype(BF16)


VMEM_SPEC = pl.BlockSpec(memory_space=pltpu.VMEM)
HBM_SPEC = pl.BlockSpec(memory_space=pltpu.HBM)
SMEM_SPEC = pl.BlockSpec(memory_space=pltpu.SMEM)


def in_hbm(x):
    return pltpu.with_memory_space_constraint(x, pltpu.HBM)


def params(mib):
    return pltpu.CompilerParams(vmem_limit_bytes=mib * 2**20)


def pairs(lats, lons, target):
    chosen = []
    for lat in range(lats):
        for lon in range(lons):
            for lev in range(2):
                to_lat, to_lon, to_lev = target(lat, lon, lev)
                chosen.append(
                    ((lat * lons + lon) * 2 + lev, (to_lat * lons + to_lon % lons) * 2 + to_lev)
                )
    return chosen


def on_device(
    levels_in,
    enc_gain,
    latent_query,
    w_query,
    w_kv,
    w_cross_out,
    shift_lat,
    shift_lon,
    attn_gain,
    w_qkv,
    w_proj,
    mlp_gain,
    w_up,
    w_down,
    merge_gain,
    w_merge,
):
    lats = lax.axis_size("lat")
    lons = lax.axis_size("lon")

    def chip(lat):
        return lat ^ 1

    def cross(lat):
        return (lat + 1) % lats if lat % 2 else (lat - 1) % lats

    def aside(lon, lev):
        return (lon - 1, 1) if lev == 0 else (lon + 1, 0)

    level_pairs = pairs(lats, lons, lambda a, o, v: (a, o, 1 - v))
    far_pairs = pairs(lats, lons, lambda a, o, v: (a, o + 1 if v == 0 else o - 1, v))
    chip_pairs = pairs(lats, lons, lambda a, o, v: (chip(a), o, v))
    def edge(a):
        return a == 0 or a == lats - 1

    cross_pairs = pairs(
        lats, lons, lambda a, o, v: (a if edge(a) else cross(a), o, 1 - v)
    )
    corner_pairs = pairs(
        lats, lons, lambda a, o, v: (a, o, 1 - v) if edge(a) else (cross(a),) + aside(o, v)
    )

    far_levels = lax.ppermute(levels_in, AXES, level_pairs)
    positions = levels_in.shape[0] * levels_in.shape[1] * levels_in.shape[2]
    kept = (w_kv, w_cross_out, w_proj, w_up, w_down, w_merge)
    scores, values, query_rows, wq_t, wv_t, wk, wkv, wcross, wproj, wup, wdown, wmerge = pl.pallas_call(
        local_kernel,
        out_shape=(
            pltpu.VMEM((positions, LATENT * HEADS), F32),
            pltpu.VMEM((positions, D), BF16),
            pltpu.VMEM((LATENT * HEADS, D), BF16),
        )
        + (pltpu.VMEM((D, D), BF16),) * 3
        + tuple(pltpu.VMEM(w.shape, BF16) for w in kept),
        in_specs=[HBM_SPEC] + [VMEM_SPEC] * 2 + [HBM_SPEC] * 8,
        out_specs=(VMEM_SPEC,) * 12,
        scratch_shapes=[
            pltpu.VMEM(levels_in.shape, BF16),
            pltpu.VMEM(w_query.shape, BF16),
            pltpu.VMEM(w_qkv.shape, BF16),
            pltpu.SemaphoreType.DMA((9,)),
        ],
        compiler_params=params(14),
        name="local_levels",
    )(
        in_hbm(levels_in), enc_gain, latent_query,
        *[in_hbm(w) for w in (w_query, w_kv, w_qkv, w_cross_out, w_proj, w_up, w_down, w_merge)],
    )
    both = pl.pallas_call(
        encode_kernel,
        out_shape=jax.ShapeDtypeStruct((2 * TOK, D), BF16),
        in_specs=[VMEM_SPEC] * 8,
        out_specs=VMEM_SPEC,
        compiler_params=params(14),
        name="encode",
    )(far_levels, scores, values, query_rows, enc_gain, latent_query, wkv, wcross)
    chip_both = lax.ppermute(both, AXES, chip_pairs)
    cross_both = lax.ppermute(both, AXES, cross_pairs)
    own, other = pl.pallas_call(
        halves_kernel,
        out_shape=(jax.ShapeDtypeStruct((TOK, D), BF16),) * 2,
        in_specs=[VMEM_SPEC, pl.BlockSpec(memory_space=pl.ANY)],
        out_specs=(VMEM_SPEC,) * 2,
        compiler_params=params(2),
        name="halves",
    )(both, chip_both)
    far = lax.ppermute(other, AXES, far_pairs)
    cross_far = lax.ppermute(own, AXES, corner_pairs)
    chip_far = lax.ppermute(far, AXES, chip_pairs)
    merged = pl.pallas_call(
        block_kernel,
        out_shape=jax.ShapeDtypeStruct((WH // 2, WW // 2, LATENT, w_merge.shape[1]), BF16),
        in_specs=[SMEM_SPEC] * 2 + [VMEM_SPEC] * 16,
        out_specs=VMEM_SPEC,
        compiler_params=params(24),
        name="window_block",
    )(
        shift_lat, shift_lon, both, far, chip_both, chip_far, cross_both, cross_far,
        attn_gain, wk, wq_t, wv_t, wproj, mlp_gain, wup, wdown, merge_gain, wmerge,
    )
    return merged.transpose(2, 0, 1, 3)


def solution(mesh):
    in_specs = (P("lev", "lat", "lon", None),) + (P(),) * 15
    out_specs = P(None, "lat", ("lon", "lev"), None)
    return jax.shard_map(
        on_device, mesh=mesh, in_specs=in_specs, out_specs=out_specs, check_vma=False
    )
```

```python
import math

import jax
import jax.numpy as jnp
from jax import lax
from jax.experimental import pallas as pl
from jax.experimental.pallas import tpu as pltpu
from jax.sharding import PartitionSpec as P

HEADS = 16
WH = 6
WW = 12
LATENT = 2
D = 512
HD = D // HEADS
TOK = LATENT * WH * WW
EPSILON = 1e-05
NEG_LARGE = -1e30
F32 = jnp.float32
BF16 = jnp.bfloat16
SCALE = 1.0 / math.sqrt(HD)
LOG2E = math.log2(math.e)
AXES = ("lat", "lon", "lev")


def layer_norm(values, gain_row):
    centre = values - jnp.mean(values, axis=-1, keepdims=True)
    spread = jnp.mean(centre * centre, axis=-1, keepdims=True)
    return centre * lax.rsqrt(spread + EPSILON) * gain_row


def dot(a, b):
    return jnp.dot(a, b, preferred_element_type=F32)


def dot_t(a, b):
    return lax.dot_general(a, b, (((1,), (1,)), ((), ())), preferred_element_type=F32)


def iota(shape, dim):
    return lax.broadcasted_iota(jnp.int32, shape, dim)


def split(index, size):
    whole = jnp.floor((index.astype(F32) + 0.5) * (1.0 / size)).astype(jnp.int32)
    return whole, index - whole * size


def token_coords(index):
    level, rest = split(index, WH * WW)
    row, col = split(rest, WW)
    return level, row, col


def row_of(ref):
    return ref[...].astype(F32).reshape(1, ref.shape[0])


def level_keyval(levels_ref, gain_row, w_kv):
    pieces = [
        levels_ref[l, r].astype(F32)
        for l in range(levels_ref.shape[0])
        for r in range(levels_ref.shape[1])
    ]
    normed = layer_norm(jnp.concatenate(pieces, axis=0), gain_row).astype(BF16)
    return dot(normed, w_kv).astype(BF16)


def local_kernel(
    shift_lat_ref, shift_lon_ref, levels_hbm, gain_hbm, lq_hbm, wq_hbm, wkv_hbm, wqkv_hbm, wcross_hbm, wproj_hbm, wup_hbm,
    wdown_hbm, wmerge_hbm,
    score_ref, value_ref, query_ref, wq_t_ref, wv_t_ref, wk_ref, wkv_ref, wcross_ref, wproj_ref,
    wup_ref, wdown_ref, wmerge_ref, shift_ref,
    gain_ref, lq_ref, levels_ref, wq_ref, wqkv_ref, sems,
):
    moves = [
        (levels_hbm, levels_ref),
        (wkv_hbm, wkv_ref),
        (wq_hbm, wq_ref),
        (wqkv_hbm, wqkv_ref),
        (wcross_hbm, wcross_ref),
        (wproj_hbm, wproj_ref),
        (wup_hbm, wup_ref),
        (wdown_hbm, wdown_ref),
        (wmerge_hbm, wmerge_ref),
        (gain_hbm, gain_ref),
        (lq_hbm, lq_ref),
    ]
    copies = [
        pltpu.make_async_copy(source, target, sems.at[i])
        for i, (source, target) in enumerate(moves)
    ]
    for copy in copies[9:] + copies[:9]:
        copy.start()
    shift_ref[...] = jnp.where(iota((8, 128), 0) == 0, shift_lat_ref[0], shift_lon_ref[0])
    for copy in copies[9:] + copies[:2]:
        copy.wait()
    keyval = level_keyval(levels_ref, row_of(gain_ref), wkv_ref[...])
    value_ref[...] = keyval[:, D:]
    copies[2].wait()
    queries = dot(lq_ref[...], wq_ref[...]).astype(BF16).astype(F32)
    rows = LATENT * HEADS
    spread = jnp.concatenate(
        [jnp.broadcast_to(queries[k : k + 1], (HEADS, D)) for k in range(LATENT)], axis=0
    )
    head_of_row = split(iota((rows, 1), 0), HEADS)[1]
    head_of_lane = split(iota((1, D), 1), HD)[0]
    query_rows = jnp.where(head_of_row == head_of_lane, spread, 0.0).astype(BF16)
    score_ref[...] = dot_t(keyval[:, :D], query_rows)
    query_ref[...] = query_rows
    copies[3].wait()
    wq_t_ref[...] = wqkv_ref[:, :D].astype(F32).T.astype(BF16)
    wk_ref[...] = wqkv_ref[:, D : 2 * D]
    wv_t_ref[...] = wqkv_ref[:, 2 * D :].astype(F32).T.astype(BF16)
    for copy in copies[4:9]:
        copy.wait()


def encode_kernel(
    levels_ref, score_ref, value_ref, query_ref, gain_ref, lq_ref, wkv_ref, wcross_ref,
    both_ref,
):
    lev = lax.axis_index("lev")
    keyval = level_keyval(levels_ref, row_of(gain_ref), wkv_ref[...])
    far_scores = dot_t(keyval[:, :D], query_ref[...])
    near_scores = score_ref[...]
    count = near_scores.shape[0] // 2
    scores = [s[i * count : (i + 1) * count] * SCALE for s in (near_scores, far_scores) for i in (0, 1)]
    top = jnp.maximum(jnp.maximum(scores[0], scores[1]), jnp.maximum(scores[2], scores[3]))
    powers = [jnp.exp(s - top) for s in scores]
    norm = 1.0 / (powers[0] + powers[1] + powers[2] + powers[3])
    weights = jnp.concatenate([p * norm for p in powers], axis=0).astype(BF16)
    lane = iota((1, LATENT * D), 1)
    expand = (iota((LATENT * HEADS, 1), 0) == split(lane, HD)[0]).astype(F32).astype(BF16)
    wide = dot(weights, expand)
    near_values = value_ref[...].astype(F32)
    far_values = keyval[:, D:].astype(F32)
    values = [x[i * count : (i + 1) * count] for x in (near_values, far_values) for i in (0, 1)]
    attended = []
    for k in range(LATENT):
        total = 0.0
        for l in range(4):
            total = total + wide[l * count : (l + 1) * count, k * D : (k + 1) * D] * values[l]
        attended.append(total.astype(BF16))
    projected = dot(jnp.concatenate(attended, axis=0), wcross_ref[...])
    query = lq_ref[...].astype(F32)
    latents = jnp.concatenate(
        [projected[k * count : (k + 1) * count] + query[k : k + 1] for k in range(LATENT)], axis=0
    ).astype(BF16)
    half, rest = split(iota((2 * TOK, 1), 0), TOK)
    level, row, col = token_coords(rest)
    side = jnp.where(half == 0, lev, 1 - lev)
    source = level * count + row * (2 * WW) + col + side * WW
    order = (iota((1, 2 * TOK), 1) == source).astype(F32).astype(BF16)
    both = dot(order, latents).astype(BF16)
    both_ref[...] = both


def halves_kernel(both_ref, chip_ref, own_ref, other_ref):
    own_ref[...] = both_ref[:TOK]
    other_ref[...] = both_ref[TOK:]


LANES = 256
PER = LANES // HD
MAIN = 128
REST = TOK - MAIN
PACKED = PER * TOK
GROUPS = D // LANES


def shifted(row, col, shift_ref):
    low_row = (row >= WH - shift_ref[0:1, 0:1]).astype(jnp.int32)
    low_col = (col >= WW - shift_ref[1:2, 0:1]).astype(jnp.int32)
    return low_row, low_col


def key_places(shift_ref):
    _, row, col = token_coords(iota((TOK, 1), 0))
    return shifted(row, col, shift_ref)


def query_places(shift_ref):
    lane = iota((1, PACKED), 1)
    token = jnp.where(
        lane < PER * MAIN, split(lane, MAIN)[1], MAIN + split(lane, REST)[1]
    )
    _, row, col = token_coords(token)
    return shifted(row, col, shift_ref)


def rest_places():
    lane = iota((1, MAIN), 1)
    head, token = split(lane, REST)
    return head, token, split(iota((LANES, 1), 0), HD)[0] == head


def near_kernel(
    shift_ref, both_ref, far_ref, chip_ref, cross_ref, gain_ref, wk_ref, wq_t_ref, wv_t_ref,
    score_ref, mark_ref, query_ref, value_ref,
):
    lat = lax.axis_index("lat")
    lev = lax.axis_index("lev")
    last_lat = lax.axis_size("lat") - 1
    row_low, col_low = key_places(shift_ref)
    own = both_ref[:TOK].astype(F32)
    beside = jnp.where(col_low == lev, both_ref[TOK:].astype(F32), far_ref[...].astype(F32))
    above = jnp.where(
        row_low == lat % 2, chip_ref[:TOK].astype(F32), cross_ref[TOK:].astype(F32)
    )
    tokens = jnp.concatenate([own, beside, above], axis=0)
    normed = layer_norm(tokens, row_of(gain_ref)).astype(BF16)
    keys = dot(normed, wk_ref[...]).astype(BF16)
    query_t = dot_t(wq_t_ref[...], normed[:TOK]).astype(BF16)

    label_row, label_col = query_places(shift_ref)
    same_row = label_row == row_low
    same_col = label_col == col_low
    outside = (~same_row) & (
        ((lat == 0) & (row_low == 1)) | ((lat == last_lat) & (row_low == 0))
    )
    bias = jnp.where(outside, NEG_LARGE, 0.0)
    mark_ref[...] = jnp.where(same_row | same_col, 1.0, bias)
    _, rest_token, rest_mask = rest_places()
    head_of_row = split(iota((LANES, 1), 0), HD)[0]
    repeat = (iota((TOK, 1), 0) == MAIN + rest_token).astype(F32).astype(BF16)
    for g in range(GROUPS):
        lo = g * LANES
        query_g = query_t[lo : lo + LANES]
        query_main = query_g[:, :MAIN].astype(F32)
        blocks = [jnp.where(head_of_row == h, query_main, 0.0).astype(BF16) for h in range(PER)]
        blocks.append(jnp.where(rest_mask, dot(query_g, repeat), 0.0).astype(BF16))
        packed = jnp.concatenate(blocks, axis=1)
        query_ref[lo : lo + LANES] = packed
        scores = dot(keys[:, lo : lo + LANES], packed)
        score_ref[g] = bias + jnp.where(
            same_row,
            jnp.where(same_col, scores[:TOK], scores[TOK : 2 * TOK]),
            scores[2 * TOK :],
        )

    _, lane_row, lane_col = token_coords(iota((1, TOK), 1))
    lane_row, lane_col = shifted(lane_row, lane_col, shift_ref)
    values = [
        dot_t(wv_t_ref[...], normed[i * TOK : (i + 1) * TOK]) for i in range(3)
    ]
    for w in range(4):
        in_row = lane_row == w // 2
        in_col = lane_col == w % 2
        window = jnp.where(
            in_row,
            jnp.where(in_col, values[0], values[1]),
            jnp.where(in_col, values[2], 0.0),
        ).astype(BF16)
        for h in range(HEADS):
            at = (h * 4 + w) * HD
            value_ref[at : at + HD] = window[h * HD : (h + 1) * HD]


def block_kernel(
    shift_ref, both_ref, chip_ref, chip_far_ref, cross_ref, cross_far_ref, score_ref, mark_ref,
    query_ref, value_ref, attn_gain_ref, wk_ref, wv_t_ref, wproj_ref, mlp_gain_ref, wup_ref,
    wdown_ref, merge_gain_ref, wmerge_ref, out_ref,
):
    lat = lax.axis_index("lat")
    lev = lax.axis_index("lev")
    row_low, col_low = key_places(shift_ref)
    use_other = col_low == lev
    corner = jnp.where(
        row_low == lat % 2,
        jnp.where(use_other, chip_ref[TOK:].astype(F32), chip_far_ref[...].astype(F32)),
        jnp.where(use_other, cross_ref[:TOK].astype(F32), cross_far_ref[...].astype(F32)),
    )
    normed = layer_norm(corner, row_of(attn_gain_ref)).astype(BF16)
    keys = dot(normed, wk_ref[...]).astype(BF16)
    corner_values = dot_t(wv_t_ref[...], normed).astype(BF16)
    _, lane_row, lane_col = token_coords(iota((1, TOK), 1))
    lane_row, lane_col = shifted(lane_row, lane_col, shift_ref)
    in_corner = [
        ((lane_row != w // 2) & (lane_col != w % 2)).astype(F32).astype(BF16) for w in range(4)
    ]
    label_row, label_col = query_places(shift_ref)
    label = label_row * 2 + label_col
    mark = mark_ref[...]
    taken = mark <= 0.0
    def pick(parts, which):
        return jnp.where(
            which < 2,
            jnp.where(which == 0, parts[0], parts[1]),
            jnp.where(which == 2, parts[2], parts[3]),
        )

    label = jnp.concatenate([label[:, :MAIN], label[:, PER * MAIN : PER * MAIN + REST]], axis=1)
    parts = []
    for g in range(GROUPS):
        lo = g * LANES
        corner_scores = dot(keys[:, lo : lo + LANES], query_ref[lo : lo + LANES])
        scores = jnp.where(taken, corner_scores + mark, score_ref[g])
        powers = jnp.exp2((scores - jnp.max(scores, axis=0, keepdims=True)) * (SCALE * LOG2E))
        weights = powers * (1.0 / jnp.sum(powers, axis=0, keepdims=True))
        rest = weights[:, PER * MAIN :]
        for h in range(PER):
            at = lo + h * HD
            mine = corner_values[at : at + HD]
            stack = value_ref[4 * at : 4 * (at + HD)] + jnp.concatenate(
                [mine * m for m in in_corner], axis=0
            )
            tail = pltpu.roll(rest, MAIN - h * REST, 1) if h else rest
            chosen = jnp.concatenate(
                [weights[:, h * MAIN : (h + 1) * MAIN], tail[:, :REST]], axis=1
            ).astype(BF16)
            result = dot(stack, chosen)
            parts.append(pick([result[w * HD : (w + 1) * HD] for w in range(4)], label))
    window_out_t = jnp.concatenate(parts, axis=0).astype(BF16)

    own = both_ref[:TOK].astype(F32)
    middle = own + lax.dot_general(
        window_out_t, wproj_ref[...], (((0,), (0,)), ((), ())), preferred_element_type=F32
    )
    mlp_in = layer_norm(middle, row_of(mlp_gain_ref)).astype(BF16)
    up = dot(mlp_in, wup_ref[...])
    inner = math.sqrt(2.0 / math.pi) * (up + 0.044715 * (up * up * up))
    hidden = (0.5 * up * (1.0 + jnp.tanh(inner))).astype(BF16)
    block_out = (middle + dot(hidden, wdown_ref[...])).astype(BF16)

    count = (WH // 2) * (WW // 2) * LATENT
    rows = (count + 7) // 8 * 8
    corner_index, place = split(iota((4 * rows, 1), 0), rows)
    pair, level = split(place, LATENT)
    row_pair, col_pair = split(pair, WW // 2)
    corner_col, corner_row = split(corner_index, 2)
    source = level * (WH * WW) + (row_pair * 2 + corner_row) * WW + col_pair * 2 + corner_col
    source = jnp.where(place < count, source, -1)
    order = (iota((1, TOK), 1) == source).astype(F32).astype(BF16)
    sorted_out = dot(order, block_out)
    grouped = jnp.concatenate([sorted_out[i * rows : (i + 1) * rows] for i in range(4)], axis=1)
    merge_in = layer_norm(grouped, row_of(merge_gain_ref)).astype(BF16)
    merged = dot(merge_in, wmerge_ref[...])
    for i in range(WH // 2):
        for j in range(WW // 2):
            start = (i * (WW // 2) + j) * LATENT
            out_ref[i, j] = merged[start : start + LATENT].astype(BF16)


VMEM_SPEC = pl.BlockSpec(memory_space=pltpu.VMEM)
HBM_SPEC = pl.BlockSpec(memory_space=pltpu.HBM)
SMEM_SPEC = pl.BlockSpec(memory_space=pltpu.SMEM)


def in_hbm(x):
    return pltpu.with_memory_space_constraint(x, pltpu.HBM)


def params(mib):
    return pltpu.CompilerParams(vmem_limit_bytes=mib * 2**20)


def pairs(lats, lons, target):
    chosen = []
    for lat in range(lats):
        for lon in range(lons):
            for lev in range(2):
                to_lat, to_lon, to_lev = target(lat, lon, lev)
                chosen.append(
                    ((lat * lons + lon) * 2 + lev, (to_lat * lons + to_lon % lons) * 2 + to_lev)
                )
    return chosen


def on_device(
    levels_in,
    enc_gain,
    latent_query,
    w_query,
    w_kv,
    w_cross_out,
    shift_lat,
    shift_lon,
    attn_gain,
    w_qkv,
    w_proj,
    mlp_gain,
    w_up,
    w_down,
    merge_gain,
    w_merge,
):
    lats = lax.axis_size("lat")
    lons = lax.axis_size("lon")

    def chip(lat):
        return lat ^ 1

    def cross(lat):
        return (lat + 1) % lats if lat % 2 else (lat - 1) % lats

    def aside(lon, lev):
        return (lon - 1, 1) if lev == 0 else (lon + 1, 0)

    level_pairs = pairs(lats, lons, lambda a, o, v: (a, o, 1 - v))
    far_pairs = pairs(lats, lons, lambda a, o, v: (a, o + 1 if v == 0 else o - 1, v))
    chip_pairs = pairs(lats, lons, lambda a, o, v: (chip(a), o, v))
    def edge(a):
        return a == 0 or a == lats - 1

    cross_pairs = pairs(
        lats, lons, lambda a, o, v: (a if edge(a) else cross(a), o, 1 - v)
    )
    corner_pairs = pairs(
        lats, lons, lambda a, o, v: (a, o, 1 - v) if edge(a) else (cross(a),) + aside(o, v)
    )

    far_levels = lax.ppermute(levels_in, AXES, level_pairs)
    positions = levels_in.shape[0] * levels_in.shape[1] * levels_in.shape[2]
    kept = (w_kv, w_cross_out, w_proj, w_up, w_down, w_merge)
    (
        scores, values, query_rows, wq_t, wv_t, wk, wkv, wcross, wproj, wup, wdown, wmerge, shifts,
    ) = pl.pallas_call(
        local_kernel,
        out_shape=(
            pltpu.VMEM((positions, LATENT * HEADS), F32),
            pltpu.VMEM((positions, D), BF16),
            pltpu.VMEM((LATENT * HEADS, D), BF16),
        )
        + (pltpu.VMEM((D, D), BF16),) * 3
        + tuple(pltpu.VMEM(w.shape, BF16) for w in kept)
        + (pltpu.VMEM((8, 128), jnp.int32),),
        in_specs=[SMEM_SPEC] * 2 + [HBM_SPEC] * 11,
        out_specs=(VMEM_SPEC,) * 13,
        scratch_shapes=[
            pltpu.VMEM(enc_gain.shape, BF16),
            pltpu.VMEM(latent_query.shape, BF16),
            pltpu.VMEM(levels_in.shape, BF16),
            pltpu.VMEM(w_query.shape, BF16),
            pltpu.VMEM(w_qkv.shape, BF16),
            pltpu.SemaphoreType.DMA((11,)),
        ],
        compiler_params=params(14),
        name="local_levels",
    )(
        shift_lat, shift_lon,
        *[
            in_hbm(x)
            for x in (
                levels_in, enc_gain, latent_query, w_query, w_kv, w_qkv, w_cross_out, w_proj, w_up,
                w_down, w_merge,
            )
        ]
    )
    both = pl.pallas_call(
        encode_kernel,
        out_shape=jax.ShapeDtypeStruct((2 * TOK, D), BF16),
        in_specs=[VMEM_SPEC] * 8,
        out_specs=VMEM_SPEC,
        compiler_params=params(14),
        name="encode",
    )(far_levels, scores, values, query_rows, enc_gain, latent_query, wkv, wcross)
    chip_both = lax.ppermute(both, AXES, chip_pairs)
    cross_both = lax.ppermute(both, AXES, cross_pairs)
    own, other = pl.pallas_call(
        halves_kernel,
        out_shape=(jax.ShapeDtypeStruct((TOK, D), BF16),) * 2,
        in_specs=[VMEM_SPEC, pl.BlockSpec(memory_space=pl.ANY)],
        out_specs=(VMEM_SPEC,) * 2,
        compiler_params=params(2),
        name="halves",
    )(both, chip_both)
    far = lax.ppermute(other, AXES, far_pairs)
    cross_far = lax.ppermute(own, AXES, corner_pairs)
    chip_far = lax.ppermute(far, AXES, chip_pairs)
    near, mark, query, value = pl.pallas_call(
        near_kernel,
        out_shape=(
            pltpu.VMEM((GROUPS, TOK, PACKED), F32),
            pltpu.VMEM((TOK, PACKED), F32),
            pltpu.VMEM((D, PACKED), BF16),
            pltpu.VMEM((4 * D, TOK), BF16),
        ),
        in_specs=[VMEM_SPEC] * 9,
        out_specs=(VMEM_SPEC,) * 4,
        compiler_params=params(14),
        name="near_windows",
    )(shifts, both, far, chip_both, cross_both, attn_gain, wk, wq_t, wv_t)
    merged = pl.pallas_call(
        block_kernel,
        out_shape=jax.ShapeDtypeStruct((WH // 2, WW // 2, LATENT, w_merge.shape[1]), BF16),
        in_specs=[VMEM_SPEC] * 19,
        out_specs=VMEM_SPEC,
        compiler_params=params(20),
        name="window_block",
    )(
        shifts, both, chip_both, chip_far, cross_both, cross_far, near, mark, query, value,
        attn_gain, wk, wv_t, wproj, mlp_gain, wup, wdown, merge_gain, wmerge,
    )
    return merged.transpose(2, 0, 1, 3)


def solution(mesh):
    in_specs = (P("lev", "lat", "lon", None),) + (P(),) * 15
    out_specs = P(None, "lat", ("lon", "lev"), None)
    return jax.shard_map(
        on_device, mesh=mesh, in_specs=in_specs, out_specs=out_specs, check_vma=False
    )
```

```python
import math

import jax
import jax.numpy as jnp
from jax import lax
from jax.experimental import pallas as pl
from jax.experimental.pallas import tpu as pltpu
from jax.sharding import PartitionSpec as P

HEADS = 16
WH = 6
WW = 12
LATENT = 2
D = 512
HD = D // HEADS
TOK = LATENT * WH * WW
EPSILON = 1e-05
NEG_LARGE = -1e30
F32 = jnp.float32
BF16 = jnp.bfloat16
SCALE = 1.0 / math.sqrt(HD)
LOG2E = math.log2(math.e)
AXES = ("lat", "lon", "lev")


def layer_norm(values, gain_row):
    centre = values - jnp.mean(values, axis=-1, keepdims=True)
    spread = jnp.mean(centre * centre, axis=-1, keepdims=True)
    return centre * lax.rsqrt(spread + EPSILON) * gain_row


def dot(a, b):
    return jnp.dot(a, b, preferred_element_type=F32)


def dot_t(a, b):
    return lax.dot_general(a, b, (((1,), (1,)), ((), ())), preferred_element_type=F32)


def iota(shape, dim):
    return lax.broadcasted_iota(jnp.int32, shape, dim)


def split(index, size):
    whole = jnp.floor((index.astype(F32) + 0.5) * (1.0 / size)).astype(jnp.int32)
    return whole, index - whole * size


def token_coords(index):
    pair, place = split(index, 2 * WW)
    level, pair = split(pair, WH // 2)
    odd = jnp.where(place < 16, place >> 3, (place >> 2) & 1)
    col = jnp.where(place < 16, place & 7, 8 + (place & 3))
    return level, 2 * pair + odd, col


def token_index(level, pair, odd, col):
    place = jnp.where(col < 8, odd * 8 + col, 8 + odd * 4 + col)
    return (level * (WH // 2) + pair) * (2 * WW) + place


def halves_of(latents):
    upper = iota((8, 1), 0) < 4
    left, right = [], []
    for start in range(0, latents.shape[0], 4 * WW):
        tiles = [latents[start + 8 * i : start + 8 * i + 8] for i in range(6)]
        turned = [pltpu.roll(tiles[i], 4, 0) if i % 3 else None for i in range(6)]
        left += [tiles[0], tiles[3], jnp.where(upper, tiles[1], turned[4])]
        right += [
            jnp.where(upper, turned[1], turned[2]),
            jnp.where(upper, turned[4], turned[5]),
            jnp.where(upper, turned[2], tiles[5]),
        ]
    return jnp.concatenate(left, axis=0), jnp.concatenate(right, axis=0)


def row_of(ref):
    return ref[...].astype(F32).reshape(1, ref.shape[0])


def level_keyval(levels_ref, gain_row, w_kv):
    pieces = [
        levels_ref[l, r].astype(F32)
        for l in range(levels_ref.shape[0])
        for r in range(levels_ref.shape[1])
    ]
    normed = layer_norm(jnp.concatenate(pieces, axis=0), gain_row).astype(BF16)
    return dot(normed, w_kv).astype(BF16)


def local_kernel(
    shift_lat_ref, shift_lon_ref, levels_hbm, gain_hbm, lq_hbm, wq_hbm, wkv_hbm, wqkv_hbm, wcross_hbm, wproj_hbm, wup_hbm,
    wdown_hbm, wmerge_hbm,
    score_ref, value_ref, query_ref, wq_t_ref, wv_t_ref, wk_ref, wkv_ref, wcross_ref, wproj_ref,
    wup_ref, wdown_ref, wmerge_ref, shift_ref,
    gain_ref, lq_ref, levels_ref, wq_ref, wqkv_ref, sems,
):
    moves = [
        (levels_hbm, levels_ref),
        (wkv_hbm, wkv_ref),
        (wq_hbm, wq_ref),
        (wqkv_hbm, wqkv_ref),
        (wcross_hbm, wcross_ref),
        (wproj_hbm, wproj_ref),
        (wup_hbm, wup_ref),
        (wdown_hbm, wdown_ref),
        (wmerge_hbm, wmerge_ref),
        (gain_hbm, gain_ref),
        (lq_hbm, lq_ref),
    ]
    copies = [
        pltpu.make_async_copy(source, target, sems.at[i])
        for i, (source, target) in enumerate(moves)
    ]
    for copy in copies[9:] + copies[:9]:
        copy.start()
    shift_ref[...] = jnp.where(iota((8, 128), 0) == 0, shift_lat_ref[0], shift_lon_ref[0])
    for copy in copies[9:] + copies[:2]:
        copy.wait()
    keyval = level_keyval(levels_ref, row_of(gain_ref), wkv_ref[...])
    value_ref[...] = keyval[:, D:]
    copies[2].wait()
    queries = dot(lq_ref[...], wq_ref[...]).astype(BF16).astype(F32)
    rows = LATENT * HEADS
    spread = jnp.concatenate(
        [jnp.broadcast_to(queries[k : k + 1], (HEADS, D)) for k in range(LATENT)], axis=0
    )
    head_of_row = split(iota((rows, 1), 0), HEADS)[1]
    head_of_lane = split(iota((1, D), 1), HD)[0]
    query_rows = jnp.where(head_of_row == head_of_lane, spread, 0.0).astype(BF16)
    score_ref[...] = dot_t(keyval[:, :D], query_rows)
    query_ref[...] = query_rows
    copies[3].wait()
    wq_t_ref[...] = wqkv_ref[:, :D].astype(F32).T.astype(BF16)
    wk_ref[...] = wqkv_ref[:, D : 2 * D]
    wv_t_ref[...] = wqkv_ref[:, 2 * D :].astype(F32).T.astype(BF16)
    for copy in copies[4:9]:
        copy.wait()


def encode_kernel(
    levels_ref, score_ref, value_ref, query_ref, gain_ref, lq_ref, wkv_ref, wcross_ref,
    both_ref,
):
    lev = lax.axis_index("lev")
    keyval = level_keyval(levels_ref, row_of(gain_ref), wkv_ref[...])
    far_scores = dot_t(keyval[:, :D], query_ref[...])
    near_scores = score_ref[...]
    count = near_scores.shape[0] // 2
    scores = [s[i * count : (i + 1) * count] * SCALE for s in (near_scores, far_scores) for i in (0, 1)]
    top = jnp.maximum(jnp.maximum(scores[0], scores[1]), jnp.maximum(scores[2], scores[3]))
    powers = [jnp.exp(s - top) for s in scores]
    norm = 1.0 / (powers[0] + powers[1] + powers[2] + powers[3])
    weights = jnp.concatenate([p * norm for p in powers], axis=0).astype(BF16)
    lane = iota((1, LATENT * D), 1)
    expand = (iota((LATENT * HEADS, 1), 0) == split(lane, HD)[0]).astype(F32).astype(BF16)
    wide = dot(weights, expand)
    near_values = value_ref[...].astype(F32)
    far_values = keyval[:, D:].astype(F32)
    values = [x[i * count : (i + 1) * count] for x in (near_values, far_values) for i in (0, 1)]
    attended = []
    for k in range(LATENT):
        total = 0.0
        for l in range(4):
            total = total + wide[l * count : (l + 1) * count, k * D : (k + 1) * D] * values[l]
        attended.append(total.astype(BF16))
    projected = dot(jnp.concatenate(attended, axis=0), wcross_ref[...])
    query = lq_ref[...].astype(F32)
    latents = jnp.concatenate(
        [projected[k * count : (k + 1) * count] + query[k : k + 1] for k in range(LATENT)], axis=0
    )
    left, right = halves_of(latents)
    first = lev == 0
    both = jnp.concatenate(
        [jnp.where(first, left, right), jnp.where(first, right, left)], axis=0
    ).astype(BF16)
    both_ref[...] = both


def halves_kernel(both_ref, chip_ref, own_ref, other_ref):
    own_ref[...] = both_ref[:TOK]
    other_ref[...] = both_ref[TOK:]


LANES = 256
PER = LANES // HD
MAIN = 128
REST = TOK - MAIN
PACKED = PER * TOK
GROUPS = D // LANES


def shifted(row, col, shift_ref):
    low_row = (row >= WH - shift_ref[0:1, 0:1]).astype(jnp.int32)
    low_col = (col >= WW - shift_ref[1:2, 0:1]).astype(jnp.int32)
    return low_row, low_col


def key_places(shift_ref):
    _, row, col = token_coords(iota((TOK, 1), 0))
    return shifted(row, col, shift_ref)


def query_places(shift_ref):
    lane = iota((1, PACKED), 1)
    token = jnp.where(
        lane < PER * MAIN, split(lane, MAIN)[1], MAIN + split(lane, REST)[1]
    )
    _, row, col = token_coords(token)
    return shifted(row, col, shift_ref)


def rest_places():
    lane = iota((1, MAIN), 1)
    head, token = split(lane, REST)
    return head, token, split(iota((LANES, 1), 0), HD)[0] == head


def near_kernel(
    shift_ref, both_ref, far_ref, chip_ref, cross_ref, gain_ref, wk_ref, wq_t_ref, wv_t_ref,
    score_ref, mark_ref, query_ref, value_ref,
):
    lat = lax.axis_index("lat")
    lev = lax.axis_index("lev")
    last_lat = lax.axis_size("lat") - 1
    row_low, col_low = key_places(shift_ref)
    own = both_ref[:TOK].astype(F32)
    beside = jnp.where(col_low == lev, both_ref[TOK:].astype(F32), far_ref[...].astype(F32))
    above = jnp.where(
        row_low == lat % 2, chip_ref[:TOK].astype(F32), cross_ref[TOK:].astype(F32)
    )
    tokens = jnp.concatenate([own, beside, above], axis=0)
    normed = layer_norm(tokens, row_of(gain_ref)).astype(BF16)
    keys = dot(normed, wk_ref[...]).astype(BF16)
    query_t = dot_t(wq_t_ref[...], normed[:TOK]).astype(BF16)

    label_row, label_col = query_places(shift_ref)
    same_row = label_row == row_low
    same_col = label_col == col_low
    outside = (~same_row) & (
        ((lat == 0) & (row_low == 1)) | ((lat == last_lat) & (row_low == 0))
    )
    bias = jnp.where(outside, NEG_LARGE, 0.0)
    mark_ref[...] = jnp.where(same_row | same_col, 1.0, bias)
    _, rest_token, rest_mask = rest_places()
    head_of_row = split(iota((LANES, 1), 0), HD)[0]
    repeat = (iota((TOK, 1), 0) == MAIN + rest_token).astype(F32).astype(BF16)
    for g in range(GROUPS):
        lo = g * LANES
        query_g = query_t[lo : lo + LANES]
        query_main = query_g[:, :MAIN].astype(F32)
        blocks = [jnp.where(head_of_row == h, query_main, 0.0).astype(BF16) for h in range(PER)]
        blocks.append(jnp.where(rest_mask, dot(query_g, repeat), 0.0).astype(BF16))
        packed = jnp.concatenate(blocks, axis=1)
        query_ref[lo : lo + LANES] = packed
        scores = dot(keys[:, lo : lo + LANES], packed)
        score_ref[g] = bias + jnp.where(
            same_row,
            jnp.where(same_col, scores[:TOK], scores[TOK : 2 * TOK]),
            scores[2 * TOK :],
        )

    _, lane_row, lane_col = token_coords(iota((1, TOK), 1))
    lane_row, lane_col = shifted(lane_row, lane_col, shift_ref)
    values = [
        dot_t(wv_t_ref[...], normed[i * TOK : (i + 1) * TOK]).astype(BF16) for i in range(3)
    ]
    for w in range(4):
        in_row = lane_row == w // 2
        in_col = lane_col == w % 2
        masks = [
            x.astype(F32).astype(BF16) for x in (in_row & in_col, in_row & ~in_col, ~in_row & in_col)
        ]
        window = values[0] * masks[0] + values[1] * masks[1] + values[2] * masks[2]
        for h in range(HEADS):
            at = (h * 4 + w) * HD
            value_ref[at : at + HD] = window[h * HD : (h + 1) * HD]


def block_kernel(
    shift_ref, both_ref, chip_ref, chip_far_ref, cross_ref, cross_far_ref, score_ref, mark_ref,
    query_ref, value_ref, attn_gain_ref, wk_ref, wv_t_ref, wproj_ref, mlp_gain_ref, wup_ref,
    wdown_ref, merge_gain_ref, wmerge_ref, out_ref,
):
    lat = lax.axis_index("lat")
    lev = lax.axis_index("lev")
    row_low, col_low = key_places(shift_ref)
    use_other = col_low == lev
    corner = jnp.where(
        row_low == lat % 2,
        jnp.where(use_other, chip_ref[TOK:].astype(F32), chip_far_ref[...].astype(F32)),
        jnp.where(use_other, cross_ref[:TOK].astype(F32), cross_far_ref[...].astype(F32)),
    )
    normed = layer_norm(corner, row_of(attn_gain_ref)).astype(BF16)
    keys = dot(normed, wk_ref[...]).astype(BF16)
    corner_values = dot_t(wv_t_ref[...], normed).astype(BF16)
    _, lane_row, lane_col = token_coords(iota((1, TOK), 1))
    lane_row, lane_col = shifted(lane_row, lane_col, shift_ref)
    in_corner = [
        ((lane_row != w // 2) & (lane_col != w % 2)).astype(F32).astype(BF16) for w in range(4)
    ]
    label_row, label_col = query_places(shift_ref)
    label = label_row * 2 + label_col
    mark = mark_ref[...]
    taken = mark <= 0.0
    def pick(parts, which):
        return jnp.where(
            which < 2,
            jnp.where(which == 0, parts[0], parts[1]),
            jnp.where(which == 2, parts[2], parts[3]),
        )

    label = jnp.concatenate([label[:, :MAIN], label[:, PER * MAIN : PER * MAIN + REST]], axis=1)
    parts = []
    for g in range(GROUPS):
        lo = g * LANES
        corner_scores = dot(keys[:, lo : lo + LANES], query_ref[lo : lo + LANES])
        scores = jnp.where(taken, corner_scores + mark, score_ref[g])
        powers = jnp.exp2((scores - jnp.max(scores, axis=0, keepdims=True)) * (SCALE * LOG2E))
        weights = powers * (1.0 / jnp.sum(powers, axis=0, keepdims=True))
        rest = weights[:, PER * MAIN :]
        for h in range(PER):
            at = lo + h * HD
            mine = corner_values[at : at + HD]
            stack = value_ref[4 * at : 4 * (at + HD)] + jnp.concatenate(
                [mine * m for m in in_corner], axis=0
            )
            tail = pltpu.roll(rest, MAIN - h * REST, 1) if h else rest
            chosen = jnp.concatenate(
                [weights[:, h * MAIN : (h + 1) * MAIN], tail[:, :REST]], axis=1
            ).astype(BF16)
            result = dot(stack, chosen)
            parts.append(pick([result[w * HD : (w + 1) * HD] for w in range(4)], label))
    window_out_t = jnp.concatenate(parts, axis=0).astype(BF16)

    own = both_ref[:TOK].astype(F32)
    middle = own + lax.dot_general(
        window_out_t, wproj_ref[...], (((0,), (0,)), ((), ())), preferred_element_type=F32
    )
    mlp_in = layer_norm(middle, row_of(mlp_gain_ref)).astype(BF16)
    up = dot(mlp_in, wup_ref[...])
    inner = math.sqrt(2.0 / math.pi) * (up + 0.044715 * (up * up * up))
    hidden = (0.5 * up * (1.0 + jnp.tanh(inner))).astype(BF16)
    block_out = (middle + dot(hidden, wdown_ref[...])).astype(BF16)

    count = (WH // 2) * (WW // 2) * LATENT
    rows = (count + 7) // 8 * 8
    corner_index, place = split(iota((4 * rows, 1), 0), rows)
    pair, level = split(place, LATENT)
    row_pair, col_pair = split(pair, WW // 2)
    corner_col, corner_row = split(corner_index, 2)
    source = token_index(level, row_pair, corner_row, col_pair * 2 + corner_col)
    source = jnp.where(place < count, source, -1)
    order = (iota((1, TOK), 1) == source).astype(F32).astype(BF16)
    sorted_out = dot(order, block_out)
    grouped = jnp.concatenate([sorted_out[i * rows : (i + 1) * rows] for i in range(4)], axis=1)
    merge_in = layer_norm(grouped, row_of(merge_gain_ref)).astype(BF16)
    merged = dot(merge_in, wmerge_ref[...])
    for i in range(WH // 2):
        for j in range(WW // 2):
            start = (i * (WW // 2) + j) * LATENT
            out_ref[i, j] = merged[start : start + LATENT].astype(BF16)


VMEM_SPEC = pl.BlockSpec(memory_space=pltpu.VMEM)
HBM_SPEC = pl.BlockSpec(memory_space=pltpu.HBM)
SMEM_SPEC = pl.BlockSpec(memory_space=pltpu.SMEM)


def in_hbm(x):
    return pltpu.with_memory_space_constraint(x, pltpu.HBM)


def params(mib):
    return pltpu.CompilerParams(vmem_limit_bytes=mib * 2**20)


def pairs(lats, lons, target):
    chosen = []
    for lat in range(lats):
        for lon in range(lons):
            for lev in range(2):
                to_lat, to_lon, to_lev = target(lat, lon, lev)
                chosen.append(
                    ((lat * lons + lon) * 2 + lev, (to_lat * lons + to_lon % lons) * 2 + to_lev)
                )
    return chosen


def on_device(
    levels_in,
    enc_gain,
    latent_query,
    w_query,
    w_kv,
    w_cross_out,
    shift_lat,
    shift_lon,
    attn_gain,
    w_qkv,
    w_proj,
    mlp_gain,
    w_up,
    w_down,
    merge_gain,
    w_merge,
):
    lats = lax.axis_size("lat")
    lons = lax.axis_size("lon")

    def chip(lat):
        return lat ^ 1

    def cross(lat):
        return (lat + 1) % lats if lat % 2 else (lat - 1) % lats

    def aside(lon, lev):
        return (lon - 1, 1) if lev == 0 else (lon + 1, 0)

    level_pairs = pairs(lats, lons, lambda a, o, v: (a, o, 1 - v))
    far_pairs = pairs(lats, lons, lambda a, o, v: (a, o + 1 if v == 0 else o - 1, v))
    chip_pairs = pairs(lats, lons, lambda a, o, v: (chip(a), o, v))
    def edge(a):
        return a == 0 or a == lats - 1

    cross_pairs = pairs(
        lats, lons, lambda a, o, v: (a if edge(a) else cross(a), o, 1 - v)
    )
    corner_pairs = pairs(
        lats, lons, lambda a, o, v: (a, o, 1 - v) if edge(a) else (cross(a),) + aside(o, v)
    )

    far_levels = lax.ppermute(levels_in, AXES, level_pairs)
    positions = levels_in.shape[0] * levels_in.shape[1] * levels_in.shape[2]
    kept = (w_kv, w_cross_out, w_proj, w_up, w_down, w_merge)
    (
        scores, values, query_rows, wq_t, wv_t, wk, wkv, wcross, wproj, wup, wdown, wmerge, shifts,
    ) = pl.pallas_call(
        local_kernel,
        out_shape=(
            pltpu.VMEM((positions, LATENT * HEADS), F32),
            pltpu.VMEM((positions, D), BF16),
            pltpu.VMEM((LATENT * HEADS, D), BF16),
        )
        + (pltpu.VMEM((D, D), BF16),) * 3
        + tuple(pltpu.VMEM(w.shape, BF16) for w in kept)
        + (pltpu.VMEM((8, 128), jnp.int32),),
        in_specs=[SMEM_SPEC] * 2 + [HBM_SPEC] * 11,
        out_specs=(VMEM_SPEC,) * 13,
        scratch_shapes=[
            pltpu.VMEM(enc_gain.shape, BF16),
            pltpu.VMEM(latent_query.shape, BF16),
            pltpu.VMEM(levels_in.shape, BF16),
            pltpu.VMEM(w_query.shape, BF16),
            pltpu.VMEM(w_qkv.shape, BF16),
            pltpu.SemaphoreType.DMA((11,)),
        ],
        compiler_params=params(14),
        name="local_levels",
    )(
        shift_lat, shift_lon,
        *[
            in_hbm(x)
            for x in (
                levels_in, enc_gain, latent_query, w_query, w_kv, w_qkv, w_cross_out, w_proj, w_up,
                w_down, w_merge,
            )
        ]
    )
    both = pl.pallas_call(
        encode_kernel,
        out_shape=jax.ShapeDtypeStruct((2 * TOK, D), BF16),
        in_specs=[VMEM_SPEC] * 8,
        out_specs=VMEM_SPEC,
        compiler_params=params(14),
        name="encode",
    )(far_levels, scores, values, query_rows, enc_gain, latent_query, wkv, wcross)
    chip_both = lax.ppermute(both, AXES, chip_pairs)
    cross_both = lax.ppermute(both, AXES, cross_pairs)
    own, other = pl.pallas_call(
        halves_kernel,
        out_shape=(jax.ShapeDtypeStruct((TOK, D), BF16),) * 2,
        in_specs=[VMEM_SPEC, pl.BlockSpec(memory_space=pl.ANY)],
        out_specs=(VMEM_SPEC,) * 2,
        compiler_params=params(2),
        name="halves",
    )(both, chip_both)
    far = lax.ppermute(other, AXES, far_pairs)
    cross_far = lax.ppermute(own, AXES, corner_pairs)
    chip_far = lax.ppermute(far, AXES, chip_pairs)
    near, mark, query, value = pl.pallas_call(
        near_kernel,
        out_shape=(
            pltpu.VMEM((GROUPS, TOK, PACKED), F32),
            pltpu.VMEM((TOK, PACKED), F32),
            pltpu.VMEM((D, PACKED), BF16),
            pltpu.VMEM((4 * D, TOK), BF16),
        ),
        in_specs=[VMEM_SPEC] * 9,
        out_specs=(VMEM_SPEC,) * 4,
        compiler_params=params(14),
        name="near_windows",
    )(shifts, both, far, chip_both, cross_both, attn_gain, wk, wq_t, wv_t)
    merged = pl.pallas_call(
        block_kernel,
        out_shape=jax.ShapeDtypeStruct((WH // 2, WW // 2, LATENT, w_merge.shape[1]), BF16),
        in_specs=[VMEM_SPEC] * 19,
        out_specs=VMEM_SPEC,
        compiler_params=params(20),
        name="window_block",
    )(
        shifts, both, chip_both, chip_far, cross_both, cross_far, near, mark, query, value,
        attn_gain, wk, wv_t, wproj, mlp_gain, wup, wdown, merge_gain, wmerge,
    )
    return merged.transpose(2, 0, 1, 3)


def solution(mesh):
    in_specs = (P("lev", "lat", "lon", None),) + (P(),) * 15
    out_specs = P(None, "lat", ("lon", "lev"), None)
    return jax.shard_map(
        on_device, mesh=mesh, in_specs=in_specs, out_specs=out_specs, check_vma=False
    )
```

```python
import math

import jax
import jax.numpy as jnp
from jax import lax
from jax.experimental import pallas as pl
from jax.experimental.pallas import tpu as pltpu
from jax.sharding import PartitionSpec as P

HEADS = 16
WH = 6
WW = 12
LATENT = 2
D = 512
HD = D // HEADS
TOK = LATENT * WH * WW
EPSILON = 1e-05
NEG_LARGE = -1e30
F32 = jnp.float32
BF16 = jnp.bfloat16
SCALE = 1.0 / math.sqrt(HD)
LOG2E = math.log2(math.e)
AXES = ("lat", "lon", "lev")


def layer_norm(values, gain_row):
    centre = values - jnp.mean(values, axis=-1, keepdims=True)
    spread = jnp.mean(centre * centre, axis=-1, keepdims=True)
    return centre * lax.rsqrt(spread + EPSILON) * gain_row


def dot(a, b):
    return jnp.dot(a, b, preferred_element_type=F32)


def dot_t(a, b):
    return lax.dot_general(a, b, (((1,), (1,)), ((), ())), preferred_element_type=F32)


def iota(shape, dim):
    return lax.broadcasted_iota(jnp.int32, shape, dim)


def split(index, size):
    whole = jnp.floor((index.astype(F32) + 0.5) * (1.0 / size)).astype(jnp.int32)
    return whole, index - whole * size


def token_coords(index):
    pair, place = split(index, 2 * WW)
    level, pair = split(pair, WH // 2)
    odd = jnp.where(place < 16, place >> 3, (place >> 2) & 1)
    col = jnp.where(place < 16, place & 7, 8 + (place & 3))
    return level, 2 * pair + odd, col


def token_index(level, pair, odd, col):
    place = jnp.where(col < 8, odd * 8 + col, 8 + odd * 4 + col)
    return (level * (WH // 2) + pair) * (2 * WW) + place


def halves_of(latents):
    upper = iota((8, 1), 0) < 4
    left, right = [], []
    for start in range(0, latents.shape[0], 4 * WW):
        tiles = [latents[start + 8 * i : start + 8 * i + 8] for i in range(6)]
        turned = [pltpu.roll(tiles[i], 4, 0) if i % 3 else None for i in range(6)]
        left += [tiles[0], tiles[3], jnp.where(upper, tiles[1], turned[4])]
        right += [
            jnp.where(upper, turned[1], turned[2]),
            jnp.where(upper, turned[4], turned[5]),
            jnp.where(upper, turned[2], tiles[5]),
        ]
    return jnp.concatenate(left, axis=0), jnp.concatenate(right, axis=0)


def row_of(ref):
    return ref[...].astype(F32).reshape(1, ref.shape[0])


def level_keyval(levels_ref, gain_row, w_kv):
    pieces = [
        levels_ref[l, r].astype(F32)
        for l in range(levels_ref.shape[0])
        for r in range(levels_ref.shape[1])
    ]
    normed = layer_norm(jnp.concatenate(pieces, axis=0), gain_row).astype(BF16)
    return dot(normed, w_kv).astype(BF16)


def local_kernel(
    shift_lat_ref, shift_lon_ref, levels_hbm, gain_hbm, lq_hbm, wq_hbm, wkv_hbm, wqkv_hbm, wcross_hbm, wproj_hbm, wup_hbm,
    wdown_hbm, wmerge_hbm,
    score_ref, value_ref, query_ref, wq_t_ref, wv_t_ref, wk_ref, wkv_ref, wcross_ref, wproj_ref,
    wup_ref, wdown_ref, wmerge_ref, shift_ref,
    gain_ref, lq_ref, levels_ref, wq_ref, wqkv_ref, sems,
):
    moves = [
        (levels_hbm, levels_ref),
        (wkv_hbm, wkv_ref),
        (wq_hbm, wq_ref),
        (wqkv_hbm, wqkv_ref),
        (wcross_hbm, wcross_ref),
        (wproj_hbm, wproj_ref),
        (wup_hbm, wup_ref),
        (wdown_hbm, wdown_ref),
        (wmerge_hbm, wmerge_ref),
        (gain_hbm, gain_ref),
        (lq_hbm, lq_ref),
    ]
    copies = [
        pltpu.make_async_copy(source, target, sems.at[i])
        for i, (source, target) in enumerate(moves)
    ]
    for copy in copies[9:] + copies[:9]:
        copy.start()
    shift_ref[...] = jnp.where(iota((8, 128), 0) == 0, shift_lat_ref[0], shift_lon_ref[0])
    for copy in copies[9:] + copies[:2]:
        copy.wait()
    keyval = level_keyval(levels_ref, row_of(gain_ref), wkv_ref[...])
    value_ref[...] = keyval[:, D:]
    copies[2].wait()
    queries = dot(lq_ref[...], wq_ref[...]).astype(BF16).astype(F32)
    rows = LATENT * HEADS
    spread = jnp.concatenate(
        [jnp.broadcast_to(queries[k : k + 1], (HEADS, D)) for k in range(LATENT)], axis=0
    )
    head_of_row = split(iota((rows, 1), 0), HEADS)[1]
    head_of_lane = split(iota((1, D), 1), HD)[0]
    query_rows = jnp.where(head_of_row == head_of_lane, spread, 0.0).astype(BF16)
    score_ref[...] = dot_t(keyval[:, :D], query_rows)
    query_ref[...] = query_rows
    copies[3].wait()
    wq_t_ref[...] = wqkv_ref[:, :D].astype(F32).T.astype(BF16)
    wk_ref[...] = wqkv_ref[:, D : 2 * D]
    wv_t_ref[...] = wqkv_ref[:, 2 * D :].astype(F32).T.astype(BF16)
    for copy in copies[4:9]:
        copy.wait()


def encode_kernel(
    levels_ref, score_ref, value_ref, query_ref, gain_ref, lq_ref, wkv_ref, wcross_ref,
    both_ref,
):
    lev = lax.axis_index("lev")
    keyval = level_keyval(levels_ref, row_of(gain_ref), wkv_ref[...])
    far_scores = dot_t(keyval[:, :D], query_ref[...])
    near_scores = score_ref[...]
    count = near_scores.shape[0] // 2
    scores = [s[i * count : (i + 1) * count] * SCALE for s in (near_scores, far_scores) for i in (0, 1)]
    top = jnp.maximum(jnp.maximum(scores[0], scores[1]), jnp.maximum(scores[2], scores[3]))
    powers = [jnp.exp(s - top) for s in scores]
    norm = 1.0 / (powers[0] + powers[1] + powers[2] + powers[3])
    weights = jnp.concatenate([p * norm for p in powers], axis=0).astype(BF16)
    lane = iota((1, LATENT * D), 1)
    expand = (iota((LATENT * HEADS, 1), 0) == split(lane, HD)[0]).astype(F32).astype(BF16)
    wide = dot(weights, expand)
    near_values = value_ref[...].astype(F32)
    far_values = keyval[:, D:].astype(F32)
    values = [x[i * count : (i + 1) * count] for x in (near_values, far_values) for i in (0, 1)]
    attended = []
    for k in range(LATENT):
        total = 0.0
        for l in range(4):
            total = total + wide[l * count : (l + 1) * count, k * D : (k + 1) * D] * values[l]
        attended.append(total.astype(BF16))
    projected = dot(jnp.concatenate(attended, axis=0), wcross_ref[...])
    query = lq_ref[...].astype(F32)
    latents = jnp.concatenate(
        [projected[k * count : (k + 1) * count] + query[k : k + 1] for k in range(LATENT)], axis=0
    )
    left, right = halves_of(latents)
    first = lev == 0
    both = jnp.concatenate(
        [jnp.where(first, left, right), jnp.where(first, right, left)], axis=0
    ).astype(BF16)
    both_ref[...] = both


def halves_kernel(both_ref, chip_ref, own_ref, other_ref):
    own_ref[...] = both_ref[:TOK]
    other_ref[...] = both_ref[TOK:]


LANES = 256
PER = LANES // HD
MAIN = 128
REST = TOK - MAIN
PACKED = PER * TOK
GROUPS = D // LANES


def shifted(row, col, shift_ref):
    low_row = (row >= WH - shift_ref[0:1, 0:1]).astype(jnp.int32)
    low_col = (col >= WW - shift_ref[1:2, 0:1]).astype(jnp.int32)
    return low_row, low_col


def key_places(shift_ref):
    _, row, col = token_coords(iota((TOK, 1), 0))
    return shifted(row, col, shift_ref)


def query_places(shift_ref):
    lane = iota((1, PACKED), 1)
    token = jnp.where(
        lane < PER * MAIN, split(lane, MAIN)[1], MAIN + split(lane, REST)[1]
    )
    _, row, col = token_coords(token)
    return shifted(row, col, shift_ref)


def rest_places():
    lane = iota((1, MAIN), 1)
    head, token = split(lane, REST)
    return head, token, split(iota((LANES, 1), 0), HD)[0] == head


def early_kernel(
    shift_ref, both_ref, chip_ref, cross_ref, gain_ref, wk_ref, wq_t_ref, wv_t_ref,
    score_ref, mark_ref, query_ref, value_ref,
):
    lat = lax.axis_index("lat")
    last_lat = lax.axis_size("lat") - 1
    row_low, col_low = key_places(shift_ref)
    own = both_ref[:TOK].astype(F32)
    above = jnp.where(
        row_low == lat % 2, chip_ref[:TOK].astype(F32), cross_ref[TOK:].astype(F32)
    )
    tokens = jnp.concatenate([own, above], axis=0)
    normed = layer_norm(tokens, row_of(gain_ref)).astype(BF16)
    keys = dot(normed, wk_ref[...]).astype(BF16)
    query_t = dot_t(wq_t_ref[...], normed[:TOK]).astype(BF16)

    label_row, label_col = query_places(shift_ref)
    same_row = label_row == row_low
    same_col = label_col == col_low
    outside = (~same_row) & (
        ((lat == 0) & (row_low == 1)) | ((lat == last_lat) & (row_low == 0))
    )
    bias = jnp.where(outside, NEG_LARGE, 0.0)
    mark_ref[...] = jnp.where(same_col, 1.0, jnp.where(same_row, 2.0, bias))
    _, rest_token, rest_mask = rest_places()
    head_of_row = split(iota((LANES, 1), 0), HD)[0]
    repeat = (iota((TOK, 1), 0) == MAIN + rest_token).astype(F32).astype(BF16)
    for g in range(GROUPS):
        lo = g * LANES
        query_g = query_t[lo : lo + LANES]
        query_main = query_g[:, :MAIN].astype(F32)
        blocks = [jnp.where(head_of_row == h, query_main, 0.0).astype(BF16) for h in range(PER)]
        blocks.append(jnp.where(rest_mask, dot(query_g, repeat), 0.0).astype(BF16))
        packed = jnp.concatenate(blocks, axis=1)
        query_ref[lo : lo + LANES] = packed
        scores = dot(keys[:, lo : lo + LANES], packed)
        score_ref[g] = bias + jnp.where(same_row, scores[:TOK], scores[TOK:])

    _, lane_row, lane_col = token_coords(iota((1, TOK), 1))
    lane_row, lane_col = shifted(lane_row, lane_col, shift_ref)
    values = [
        dot_t(wv_t_ref[...], normed[i * TOK : (i + 1) * TOK]) for i in range(2)
    ]
    for w in range(4):
        window = jnp.where(lane_row == w // 2, values[0], values[1])
        window = jnp.where(lane_col == w % 2, window, 0.0).astype(BF16)
        for h in range(HEADS):
            at = (h * 4 + w) * HD
            value_ref[at : at + HD] = window[h * HD : (h + 1) * HD]


def relay_kernel(far_ref, mark_ref, out_ref):
    out_ref[...] = far_ref[...]


def beside_kernel(
    shift_ref, both_ref, far_ref, score_in_ref, mark_ref, query_ref, value_in_ref, gain_ref,
    wk_ref, wv_t_ref, score_ref, value_ref,
):
    lev = lax.axis_index("lev")
    _, col_low = key_places(shift_ref)
    beside = jnp.where(col_low == lev, both_ref[TOK:].astype(F32), far_ref[...].astype(F32))
    normed = layer_norm(beside, row_of(gain_ref)).astype(BF16)
    keys = dot(normed, wk_ref[...]).astype(BF16)
    taken = mark_ref[...] == 2.0
    for g in range(GROUPS):
        lo = g * LANES
        scores = dot(keys[:, lo : lo + LANES], query_ref[lo : lo + LANES])
        score_ref[g] = jnp.where(taken, scores, score_in_ref[g])
    values = dot_t(wv_t_ref[...], normed).astype(BF16)
    _, lane_row, lane_col = token_coords(iota((1, TOK), 1))
    lane_row, lane_col = shifted(lane_row, lane_col, shift_ref)
    masks = [
        ((lane_row == w // 2) & (lane_col != w % 2)).astype(F32).astype(BF16) for w in range(4)
    ]
    for h in range(HEADS):
        mine = values[h * HD : (h + 1) * HD]
        for w in range(4):
            at = (h * 4 + w) * HD
            value_ref[at : at + HD] = value_in_ref[at : at + HD] + mine * masks[w]


def block_kernel(
    shift_ref, both_ref, chip_ref, chip_far_ref, cross_ref, cross_far_ref, score_ref, mark_ref,
    query_ref, value_ref, attn_gain_ref, wk_ref, wv_t_ref, wproj_ref, mlp_gain_ref, wup_ref,
    wdown_ref, merge_gain_ref, wmerge_ref, out_ref,
):
    lat = lax.axis_index("lat")
    lev = lax.axis_index("lev")
    row_low, col_low = key_places(shift_ref)
    use_other = col_low == lev
    corner = jnp.where(
        row_low == lat % 2,
        jnp.where(use_other, chip_ref[TOK:].astype(F32), chip_far_ref[...].astype(F32)),
        jnp.where(use_other, cross_ref[:TOK].astype(F32), cross_far_ref[...].astype(F32)),
    )
    normed = layer_norm(corner, row_of(attn_gain_ref)).astype(BF16)
    keys = dot(normed, wk_ref[...]).astype(BF16)
    corner_values = dot_t(wv_t_ref[...], normed).astype(BF16)
    _, lane_row, lane_col = token_coords(iota((1, TOK), 1))
    lane_row, lane_col = shifted(lane_row, lane_col, shift_ref)
    in_corner = [
        ((lane_row != w // 2) & (lane_col != w % 2)).astype(F32).astype(BF16) for w in range(4)
    ]
    label_row, label_col = query_places(shift_ref)
    label = label_row * 2 + label_col
    mark = mark_ref[...]
    taken = mark <= 0.0
    def pick(parts, which):
        return jnp.where(
            which < 2,
            jnp.where(which == 0, parts[0], parts[1]),
            jnp.where(which == 2, parts[2], parts[3]),
        )

    label = jnp.concatenate([label[:, :MAIN], label[:, PER * MAIN : PER * MAIN + REST]], axis=1)
    parts = []
    for g in range(GROUPS):
        lo = g * LANES
        corner_scores = dot(keys[:, lo : lo + LANES], query_ref[lo : lo + LANES])
        scores = jnp.where(taken, corner_scores + mark, score_ref[g])
        powers = jnp.exp2((scores - jnp.max(scores, axis=0, keepdims=True)) * (SCALE * LOG2E))
        weights = powers * (1.0 / jnp.sum(powers, axis=0, keepdims=True))
        rest = weights[:, PER * MAIN :]
        for h in range(PER):
            at = lo + h * HD
            mine = corner_values[at : at + HD]
            stack = value_ref[4 * at : 4 * (at + HD)] + jnp.concatenate(
                [mine * m for m in in_corner], axis=0
            )
            tail = pltpu.roll(rest, MAIN - h * REST, 1) if h else rest
            chosen = jnp.concatenate(
                [weights[:, h * MAIN : (h + 1) * MAIN], tail[:, :REST]], axis=1
            ).astype(BF16)
            result = dot(stack, chosen)
            parts.append(pick([result[w * HD : (w + 1) * HD] for w in range(4)], label))
    window_out_t = jnp.concatenate(parts, axis=0).astype(BF16)

    own = both_ref[:TOK].astype(F32)
    middle = own + lax.dot_general(
        window_out_t, wproj_ref[...], (((0,), (0,)), ((), ())), preferred_element_type=F32
    )
    mlp_in = layer_norm(middle, row_of(mlp_gain_ref)).astype(BF16)
    up = dot(mlp_in, wup_ref[...])
    inner = math.sqrt(2.0 / math.pi) * (up + 0.044715 * (up * up * up))
    hidden = (0.5 * up * (1.0 + jnp.tanh(inner))).astype(BF16)
    block_out = (middle + dot(hidden, wdown_ref[...])).astype(BF16)

    count = (WH // 2) * (WW // 2) * LATENT
    rows = (count + 7) // 8 * 8
    corner_index, place = split(iota((4 * rows, 1), 0), rows)
    pair, level = split(place, LATENT)
    row_pair, col_pair = split(pair, WW // 2)
    corner_col, corner_row = split(corner_index, 2)
    source = token_index(level, row_pair, corner_row, col_pair * 2 + corner_col)
    source = jnp.where(place < count, source, -1)
    order = (iota((1, TOK), 1) == source).astype(F32).astype(BF16)
    sorted_out = dot(order, block_out)
    grouped = jnp.concatenate([sorted_out[i * rows : (i + 1) * rows] for i in range(4)], axis=1)
    merge_in = layer_norm(grouped, row_of(merge_gain_ref)).astype(BF16)
    merged = dot(merge_in, wmerge_ref[...])
    for i in range(WH // 2):
        for j in range(WW // 2):
            start = (i * (WW // 2) + j) * LATENT
            out_ref[i, j] = merged[start : start + LATENT].astype(BF16)


VMEM_SPEC = pl.BlockSpec(memory_space=pltpu.VMEM)
HBM_SPEC = pl.BlockSpec(memory_space=pltpu.HBM)
SMEM_SPEC = pl.BlockSpec(memory_space=pltpu.SMEM)


def in_hbm(x):
    return pltpu.with_memory_space_constraint(x, pltpu.HBM)


def params(mib):
    return pltpu.CompilerParams(vmem_limit_bytes=mib * 2**20)


def pairs(lats, lons, target):
    chosen = []
    for lat in range(lats):
        for lon in range(lons):
            for lev in range(2):
                to_lat, to_lon, to_lev = target(lat, lon, lev)
                chosen.append(
                    ((lat * lons + lon) * 2 + lev, (to_lat * lons + to_lon % lons) * 2 + to_lev)
                )
    return chosen


def on_device(
    levels_in,
    enc_gain,
    latent_query,
    w_query,
    w_kv,
    w_cross_out,
    shift_lat,
    shift_lon,
    attn_gain,
    w_qkv,
    w_proj,
    mlp_gain,
    w_up,
    w_down,
    merge_gain,
    w_merge,
):
    lats = lax.axis_size("lat")
    lons = lax.axis_size("lon")

    def chip(lat):
        return lat ^ 1

    def cross(lat):
        return (lat + 1) % lats if lat % 2 else (lat - 1) % lats

    def aside(lon, lev):
        return (lon - 1, 1) if lev == 0 else (lon + 1, 0)

    level_pairs = pairs(lats, lons, lambda a, o, v: (a, o, 1 - v))
    far_pairs = pairs(lats, lons, lambda a, o, v: (a, o + 1 if v == 0 else o - 1, v))
    chip_pairs = pairs(lats, lons, lambda a, o, v: (chip(a), o, v))
    def edge(a):
        return a == 0 or a == lats - 1

    cross_pairs = pairs(
        lats, lons, lambda a, o, v: (a if edge(a) else cross(a), o, 1 - v)
    )
    corner_pairs = pairs(
        lats, lons, lambda a, o, v: (a, o, 1 - v) if edge(a) else (cross(a),) + aside(o, v)
    )

    far_levels = lax.ppermute(levels_in, AXES, level_pairs)
    positions = levels_in.shape[0] * levels_in.shape[1] * levels_in.shape[2]
    kept = (w_kv, w_cross_out, w_proj, w_up, w_down, w_merge)
    (
        scores, values, query_rows, wq_t, wv_t, wk, wkv, wcross, wproj, wup, wdown, wmerge, shifts,
    ) = pl.pallas_call(
        local_kernel,
        out_shape=(
            pltpu.VMEM((positions, LATENT * HEADS), F32),
            pltpu.VMEM((positions, D), BF16),
            pltpu.VMEM((LATENT * HEADS, D), BF16),
        )
        + (pltpu.VMEM((D, D), BF16),) * 3
        + tuple(pltpu.VMEM(w.shape, BF16) for w in kept)
        + (pltpu.VMEM((8, 128), jnp.int32),),
        in_specs=[SMEM_SPEC] * 2 + [HBM_SPEC] * 11,
        out_specs=(VMEM_SPEC,) * 13,
        scratch_shapes=[
            pltpu.VMEM(enc_gain.shape, BF16),
            pltpu.VMEM(latent_query.shape, BF16),
            pltpu.VMEM(levels_in.shape, BF16),
            pltpu.VMEM(w_query.shape, BF16),
            pltpu.VMEM(w_qkv.shape, BF16),
            pltpu.SemaphoreType.DMA((11,)),
        ],
        compiler_params=params(14),
        name="local_levels",
    )(
        shift_lat, shift_lon,
        *[
            in_hbm(x)
            for x in (
                levels_in, enc_gain, latent_query, w_query, w_kv, w_qkv, w_cross_out, w_proj, w_up,
                w_down, w_merge,
            )
        ]
    )
    both = pl.pallas_call(
        encode_kernel,
        out_shape=jax.ShapeDtypeStruct((2 * TOK, D), BF16),
        in_specs=[VMEM_SPEC] * 8,
        out_specs=VMEM_SPEC,
        compiler_params=params(14),
        name="encode",
    )(far_levels, scores, values, query_rows, enc_gain, latent_query, wkv, wcross)
    chip_both = lax.ppermute(both, AXES, chip_pairs)
    cross_both = lax.ppermute(both, AXES, cross_pairs)
    own, other = pl.pallas_call(
        halves_kernel,
        out_shape=(jax.ShapeDtypeStruct((TOK, D), BF16),) * 2,
        in_specs=[VMEM_SPEC, pl.BlockSpec(memory_space=pl.ANY)],
        out_specs=(VMEM_SPEC,) * 2,
        compiler_params=params(2),
        name="halves",
    )(both, chip_both)
    far = lax.ppermute(other, AXES, far_pairs)
    cross_far = lax.ppermute(own, AXES, corner_pairs)
    score_type = pltpu.VMEM((GROUPS, TOK, PACKED), F32)
    value_type = pltpu.VMEM((4 * D, TOK), BF16)
    early, mark, query, early_value = pl.pallas_call(
        early_kernel,
        out_shape=(
            score_type,
            pltpu.VMEM((TOK, PACKED), F32),
            pltpu.VMEM((D, PACKED), BF16),
            value_type,
        ),
        in_specs=[VMEM_SPEC] * 8,
        out_specs=(VMEM_SPEC,) * 4,
        compiler_params=params(14),
        name="early_windows",
    )(shifts, both, chip_both, cross_both, attn_gain, wk, wq_t, wv_t)
    far = pl.pallas_call(
        relay_kernel,
        out_shape=jax.ShapeDtypeStruct((TOK, D), BF16),
        in_specs=[VMEM_SPEC, pl.BlockSpec(memory_space=pl.ANY)],
        out_specs=VMEM_SPEC,
        compiler_params=params(2),
        name="relay",
    )(far, mark)
    chip_far = lax.ppermute(far, AXES, chip_pairs)
    near, value = pl.pallas_call(
        beside_kernel,
        out_shape=(score_type, value_type),
        in_specs=[VMEM_SPEC] * 10,
        out_specs=(VMEM_SPEC,) * 2,
        compiler_params=params(14),
        name="beside_windows",
    )(shifts, both, far, early, mark, query, early_value, attn_gain, wk, wv_t)
    merged = pl.pallas_call(
        block_kernel,
        out_shape=jax.ShapeDtypeStruct((WH // 2, WW // 2, LATENT, w_merge.shape[1]), BF16),
        in_specs=[VMEM_SPEC] * 19,
        out_specs=VMEM_SPEC,
        compiler_params=params(20),
        name="window_block",
    )(
        shifts, both, chip_both, chip_far, cross_both, cross_far, near, mark, query, value,
        attn_gain, wk, wv_t, wproj, mlp_gain, wup, wdown, merge_gain, wmerge,
    )
    return merged.transpose(2, 0, 1, 3)


def solution(mesh):
    in_specs = (P("lev", "lat", "lon", None),) + (P(),) * 15
    out_specs = P(None, "lat", ("lon", "lev"), None)
    return jax.shard_map(
        on_device, mesh=mesh, in_specs=in_specs, out_specs=out_specs, check_vma=False
    )
```
